768 devices in a mesh: outer: 12 (over z), inner: 64 (over x, y, core).
Axes of the slice: x: 4, y: 8, z: 12, core: 2. Of those that a mesh axis runs over, the one named last changes fastest.
Arguments:
- queries: bfloat16 [196608, 1024], P(('outer', 'inner')), may hold values from -60 to 60
- key_states: bfloat16 [196608, 128], P(('outer', 'inner')), may hold values from -6 to 6
- value_states: bfloat16 [196608, 128], P(('outer', 'inner')), may hold values from -6 to 6
- grad_output: bfloat16 [196608, 1024], P(('outer', 'inner')), may hold values from -6 to 6
- documents: int32 [196608], replicated, may hold values from 0 to 511, never falling along the last dimension, each value on 1 to 768 neighbouring positions
- block_order: int32 [1536], replicated, may hold values from 0 to 1535, as said below
Outputs:
- grad_queries: bfloat16 [196608, 1024], P(('outer', 'inner'))
- grad_keys: bfloat16 [196608, 128], P(('outer', 'inner'))
- grad_values: bfloat16 [196608, 128], P(('outer', 'inner'))
The draws below stay inside these ranges and needn't reach their ends.
Inputs may be any that keep to these rules, and one draw needn't show every extreme that they name: `documents`: never falling along the sequence; every document has 1 to 768 positions and one has exactly 768. `block_order`: device d of the joined index outer, inner (d = outer * 64 + inner) holds stored blocks 2 * d and 2 * d + 1, which are sequence blocks d and 1535 - d in either order.
All inputs are finite; a program needn't handle non-finite values.
Results may differ from the reference program's by a relative error of at most 0.0049.
Values may be sent and summed in bfloat16 or wider, within the bound.
A program may use at most 32 MiB of HBM per device.

```python
import math
import jax
import jax.numpy as jnp
import numpy as np
from jax import lax

D_HEAD = 128
HEADS = 8
REACH = 6
BLK = 128
DOC_MOST = 768
BLOCKS = 1536
TOKENS = 196608


def attention_draws(key):
    base_key = jax.random.fold_in(key, 29)
    key_draw, query_draw = jax.random.split(base_key, 2)
    key_rows = jnp.clip(jax.random.normal(key_draw, (TOKENS, D_HEAD), jnp.float32), -6.0, 6.0)
    query_rows = jnp.clip(jax.random.normal(query_draw, (TOKENS, HEADS, D_HEAD), jnp.float32), -6.0, 6.0)
    return (key_rows, query_rows.reshape(TOKENS, HEADS * D_HEAD))


def draw_queries(key, part):
    return attention_draws(key)[1].astype(jnp.bfloat16)


def draw_key_states(key, part):
    return attention_draws(key)[0].astype(jnp.bfloat16)


def draw_block_order(key, part):
    half_count = BLOCKS // 2
    swapped = jax.random.randint(jax.random.fold_in(key, 7), (half_count,), 0, 2, dtype=jnp.int32)
    lower_half = jnp.arange(half_count, dtype=jnp.int32)
    upper_half = BLOCKS - 1 - lower_half
    slot_zero = jnp.where(swapped == 1, upper_half, lower_half)
    slot_one = jnp.where(swapped == 1, lower_half, upper_half)
    return jnp.stack([slot_zero, slot_one], 1).reshape(BLOCKS).astype(jnp.int32)


def levels(key, extent, shards, smallest, largest):
    level = 1.0
    for dim, parts in shards:
        steps = jax.random.uniform(jax.random.fold_in(jax.random.fold_in(key, 6), dim), (parts,), jnp.float32, smallest / len(shards), largest / len(shards))
        level = level * jnp.repeat(jnp.exp(steps), extent[dim] // parts).reshape((-1,) + (1,) * (len(extent) - 1 - dim))
    return level


def profile(amount, total, reach, lean):
    loads = [(1 << 20) // math.isqrt(rank ** lean) + 1 for rank in range(2, amount + 1)]
    rest, given = total - reach - (amount - 1), [1] * (amount - 1)
    while rest > 0:
        movable = [i for i in range(amount - 1) if given[i] < reach]
        pool, remaining = sum([loads[i] for i in movable]), rest
        for i in movable:
            addition = min(reach - given[i], max(1, remaining * loads[i] // pool), rest)
            given[i] = given[i] + addition
            rest = rest - addition
    return np.array([reach] + given)


def uneven(key, number_of, total, most, lean):
    if number_of == 2:
        one = jax.random.randint(key, (), max(1, total - most), min(most, total - 1) + 1)
        return jnp.stack([one, total - one])
    sizes = jnp.asarray(profile(number_of, total, most, lean), jnp.int32)
    twos = (number_of - 1) // 2
    source_of, sink = sizes[1:1 + 2 * twos:2], sizes[2:2 + 2 * twos:2]
    room = jnp.minimum(source_of - 1, most - sink)
    passed = jax.random.randint(jax.random.fold_in(key, 1), (twos,), 0, 1 << 20) % (room + 1)
    sizes = sizes.at[1:1 + 2 * twos:2].set(source_of - passed).at[2:2 + 2 * twos:2].set(sink + passed)
    return sizes[jax.random.permutation(jax.random.fold_in(key, 2), number_of)]


def normal_values(stream_key, shape, width, bound, shards=(), kind=jnp.bfloat16):
    array = width * jax.random.normal(stream_key, shape, jnp.float32)
    if shards:
        array = array * levels(stream_key, shape, shards, -0.22, 0.18)
    return jnp.clip(array, -bound, bound).astype(kind)


def setup_inputs(seed: int = 0) -> dict:
    streams_of = jax.random.split(jax.random.key(seed), 7)
    return {
        "queries": draw_queries(jax.random.fold_in(streams_of[6], 71), 0),
        "key_states": draw_key_states(jax.random.fold_in(streams_of[6], 71), 0),
        "value_states": normal_values(streams_of[2], (TOKENS, D_HEAD), 1.0, 6.0, ((0, 768),)),
        "grad_output": normal_values(streams_of[3], (TOKENS, HEADS * D_HEAD), 1.0, 6.0, ((0, 768),)),
        "documents": jnp.searchsorted(jnp.cumsum(uneven(streams_of[4], 2 * BLOCKS // REACH, TOKENS, DOC_MOST, 2)), jnp.arange(TOKENS), side="right").astype(jnp.int32),
        "block_order": draw_block_order(jax.random.fold_in(streams_of[6], 71), 0),
    }


NEGATIVE = -1e+30

def rounded(values):
    return lax.optimization_barrier(values.astype(jnp.bfloat16)).astype(jnp.float32)

def to_sequence(stored, block_order):
    blocks = stored.reshape(BLOCKS, BLK, stored.shape[1])
    return jnp.zeros_like(blocks).at[block_order].set(blocks).reshape(stored.shape)

def to_stored(sequence, block_order):
    blocks = sequence.reshape(BLOCKS, BLK, sequence.shape[1])
    return blocks[block_order].reshape(sequence.shape)

def reference(queries, key_states, value_states, grad_output, documents, block_order):
    factor = 1.0 / math.sqrt(D_HEAD)
    pad_rows = REACH * BLK
    window_rows = (REACH + 1) * BLK
    ordered_queries = to_sequence(queries, block_order).reshape(TOKENS, HEADS, D_HEAD)
    ordered_outputs = to_sequence(grad_output, block_order).reshape(TOKENS, HEADS, D_HEAD)
    ordered_keys = to_sequence(key_states, block_order)
    ordered_values = to_sequence(value_states, block_order)
    early_keys = jnp.concatenate([jnp.zeros((pad_rows, D_HEAD), ordered_keys.dtype), ordered_keys], 0)
    early_values = jnp.concatenate([jnp.zeros((pad_rows, D_HEAD), ordered_values.dtype), ordered_values], 0)
    early_owner = jnp.concatenate([jnp.full((pad_rows,), -1, jnp.int32), documents], 0)
    block_offsets = jnp.arange(BLK, dtype=jnp.int32)
    window_offsets = jnp.arange(window_rows, dtype=jnp.int32)

    def query_block(block_index):
        row_start = (block_index * BLK).astype(jnp.int32)
        query_rows = lax.dynamic_slice_in_dim(ordered_queries, row_start, BLK, 0).astype(jnp.float32)
        output_rows = lax.dynamic_slice_in_dim(ordered_outputs, row_start, BLK, 0).astype(jnp.float32)
        key_window = lax.dynamic_slice_in_dim(early_keys, row_start, window_rows, 0).astype(jnp.float32)
        value_window = lax.dynamic_slice_in_dim(early_values, row_start, window_rows, 0).astype(jnp.float32)
        query_owner = lax.dynamic_slice_in_dim(documents, row_start, BLK, 0)
        key_owner = lax.dynamic_slice_in_dim(early_owner, row_start, window_rows, 0)
        query_place = row_start + block_offsets
        key_place = row_start - pad_rows + window_offsets
        allowed = (key_place[None, :] <= query_place[:, None]) & (key_place[None, :] >= 0) & (key_owner[None, :] == query_owner[:, None])
        scores = jnp.einsum('bhd,wd->hbw', query_rows, key_window) * factor
        grad_prob = jnp.einsum('bhd,wd->hbw', output_rows, value_window)
        masked = jnp.where(allowed[None], scores, NEGATIVE)
        top_score = masked.max(-1)
        weights = jnp.where(allowed[None], jnp.exp(scores - top_score[..., None]), 0.0)
        log_totals = top_score + jnp.log(weights.sum(-1))
        probabilities = jnp.where(allowed[None], jnp.exp(scores - log_totals[..., None]), 0.0)
        row_dots = (probabilities * grad_prob).sum(-1)
        grad_scores = rounded(probabilities * (grad_prob - row_dots[..., None]))
        grad_rows = jnp.einsum('hbw,wd->bhd', grad_scores, key_window) * factor
        return (grad_rows.astype(jnp.bfloat16).reshape(BLK, HEADS * D_HEAD), log_totals.T, row_dots.T)
    grad_blocks, total_blocks, dot_blocks = lax.map(query_block, jnp.arange(BLOCKS, dtype=jnp.int32))
    grad_query_rows = grad_blocks.reshape(TOKENS, HEADS * D_HEAD)
    log_all = total_blocks.reshape(TOKENS, HEADS)
    dots_all = dot_blocks.reshape(TOKENS, HEADS)
    late_queries = jnp.concatenate([ordered_queries, jnp.zeros((pad_rows, HEADS, D_HEAD), ordered_queries.dtype)], 0)
    late_outputs = jnp.concatenate([ordered_outputs, jnp.zeros((pad_rows, HEADS, D_HEAD), ordered_outputs.dtype)], 0)
    late_totals = jnp.concatenate([log_all, jnp.zeros((pad_rows, HEADS), log_all.dtype)], 0)
    late_dots = jnp.concatenate([dots_all, jnp.zeros((pad_rows, HEADS), dots_all.dtype)], 0)
    late_owner = jnp.concatenate([documents, jnp.full((pad_rows,), -2, jnp.int32)], 0)

    def key_block(block_index):
        row_start = (block_index * BLK).astype(jnp.int32)
        key_rows = lax.dynamic_slice_in_dim(ordered_keys, row_start, BLK, 0).astype(jnp.float32)
        value_rows = lax.dynamic_slice_in_dim(ordered_values, row_start, BLK, 0).astype(jnp.float32)
        query_window = lax.dynamic_slice_in_dim(late_queries, row_start, window_rows, 0).astype(jnp.float32)
        output_window = lax.dynamic_slice_in_dim(late_outputs, row_start, window_rows, 0).astype(jnp.float32)
        total_window = lax.dynamic_slice_in_dim(late_totals, row_start, window_rows, 0)
        dot_window = lax.dynamic_slice_in_dim(late_dots, row_start, window_rows, 0)
        key_owner = lax.dynamic_slice_in_dim(documents, row_start, BLK, 0)
        query_owner = lax.dynamic_slice_in_dim(late_owner, row_start, window_rows, 0)
        key_place = row_start + block_offsets
        query_place = row_start + window_offsets
        allowed = (key_place[None, :] <= query_place[:, None]) & (query_place[:, None] < TOKENS) & (query_owner[:, None] == key_owner[None, :])
        scores = jnp.einsum('whd,bd->hwb', query_window, key_rows) * factor
        grad_prob = jnp.einsum('whd,bd->hwb', output_window, value_rows)
        probabilities = jnp.where(allowed[None], jnp.exp(scores - total_window.T[..., None]), 0.0)
        grad_scores = probabilities * (grad_prob - dot_window.T[..., None])
        value_grads = jnp.einsum('hwb,whd->bd', rounded(probabilities), output_window)
        key_grads = jnp.einsum('hwb,whd->bd', rounded(grad_scores), query_window) * factor
        return (key_grads.astype(jnp.bfloat16), value_grads.astype(jnp.bfloat16))
    key_blocks, value_blocks = lax.map(key_block, jnp.arange(BLOCKS, dtype=jnp.int32))
    grad_key_rows = key_blocks.reshape(TOKENS, D_HEAD)
    grad_value_rows = value_blocks.reshape(TOKENS, D_HEAD)
    return (to_stored(grad_query_rows, block_order), to_stored(grad_key_rows, block_order), to_stored(grad_value_rows, block_order))
```

```python
import functools
import math

import jax
import jax.numpy as jnp
from jax import lax
from jax.experimental import pallas as pl
from jax.experimental.pallas import tpu as pltpu
from jax.sharding import PartitionSpec as P

BLK = 128
PAIR = 2 * BLK
D = 128
HEADS = 8
WIDE = HEADS * D
COLS = 2 * HEADS * BLK
NEGATIVE = -1e30
FACTOR = 1.0 / math.sqrt(D)
TO_EXP2 = FACTOR * math.log2(math.e)
MESH = pl.DeviceIdType.MESH
F32 = jnp.float32
BF16 = jnp.bfloat16


def dot_last(a, b):
    return lax.dot_general(a, b, (((1,), (1,)), ((), ())), preferred_element_type=F32)


def dot_mid(a, b):
    return lax.dot_general(a, b, (((1,), (0,)), ((), ())), preferred_element_type=F32)


def rows_of(j, half):
    if j == 0 and half == 1:
        return BLK, BLK
    if j == 3 and half == 0:
        return 0, BLK
    return 0, PAIR


def kernel(
    count,
    inner,
    order_ref,
    docs_ref,
    q_ref,
    k_ref,
    v_ref,
    do_ref,
    dq_ref,
    dk_ref,
    dv_ref,
    q_in,
    do_in,
    k_in,
    v_in,
    docs_in,
    q_all,
    do_all,
    q_other,
    do_other,
    kv,
    kv_other,
    bias,
    weights,
    grad_prob,
    st_max,
    st_sum,
    st_dot,
    st_scale,
    st_row,
    probs,
    grads,
    key_t,
    g_send,
    g_mine,
    g_other,
    own_grad,
    sib_send,
    sib_recv,
    dq_send,
    dq_recv,
    dq_mine,
    in_sem,
    kv_send_sem,
    kv_recv_sem,
    sib_send_sem,
    sib_recv_sem,
    g_send_sem,
    g_recv_sem,
):
    device = lax.axis_index("outer") * inner + lax.axis_index("inner")
    chip = lax.div(device, 2)
    core = lax.rem(device, 2)
    worker = chip + core * (count - 1 - 2 * chip)
    mirror = count - 1 - worker

    def place(u):
        u = lax.rem(u + count, count)
        upper = lax.div(u, count // 2)
        return 2 * u + upper * (2 * count - 1 - 4 * u)

    def coords(dev):
        return (lax.div(dev, inner), lax.rem(dev, inner))

    after = [place(worker + k) for k in (1, 2, 3)]
    before = [place(worker - k) for k in (1, 2, 3)]
    across = [place(mirror + k) for k in (1, 2, 3)]
    sibling = place(mirror)

    first_row = jnp.maximum(2 * worker - 6, 0)
    loads = [
        pltpu.make_async_copy(k_ref, k_in, in_sem.at[0]),
        pltpu.make_async_copy(v_ref, v_in, in_sem.at[1]),
        pltpu.make_async_copy(q_ref, q_in, in_sem.at[2]),
        pltpu.make_async_copy(do_ref, do_in, in_sem.at[3]),
        pltpu.make_async_copy(docs_ref.at[pl.ds(first_row, 8)], docs_in, in_sem.at[4]),
    ]
    for load in loads:
        load.start()

    barrier = pltpu.get_barrier_semaphore()
    for dev in after + before + [sibling]:
        pl.semaphore_signal(barrier, inc=1, device_id=coords(dev), device_id_type=MESH)
    for dev in across:

        @pl.when(dev != device)
        def _():
            pl.semaphore_signal(barrier, inc=1, device_id=coords(dev), device_id_type=MESH)

    own_hits = sum((dev == device).astype(jnp.int32) for dev in across)

    slot_zero = order_ref[2 * device]
    low_first = (slot_zero < count).astype(jnp.int32)
    keeps_zero = jnp.full((8, 128), low_first + core) == 1

    def choose(first, second):
        flat = keeps_zero[:1, :1]
        return jnp.where(flat, first, second), jnp.where(flat, second, first)

    loads[0].wait()
    mine, other = choose(k_in[:BLK], k_in[BLK:])
    kv[3 * PAIR : 3 * PAIR + BLK, :D] = mine
    kv_other[:, :D] = other
    loads[1].wait()
    mine, other = choose(v_in[:BLK], v_in[BLK:])
    kv[3 * PAIR : 3 * PAIR + BLK, D:] = mine
    kv_other[:, D:] = other

    pl.semaphore_wait(barrier, 10 - own_hits)

    def kv_mine_copy(k):
        start = (3 - k) * PAIR
        return pltpu.make_async_remote_copy(
            src_ref=kv.at[pl.ds(3 * PAIR, BLK)],
            dst_ref=kv.at[pl.ds(start, BLK)],
            send_sem=kv_send_sem.at[2 * k],
            recv_sem=kv_recv_sem.at[2 * k],
            device_id=coords(after[k - 1]),
            device_id_type=MESH,
        )

    def kv_other_copy(k):
        start = (3 - k) * PAIR + BLK
        return pltpu.make_async_remote_copy(
            src_ref=kv_other,
            dst_ref=kv.at[pl.ds(start, BLK)],
            send_sem=kv_send_sem.at[2 * k + 1],
            recv_sem=kv_recv_sem.at[2 * k + 1],
            device_id=coords(across[k - 1] if k else sibling),
            device_id_type=MESH,
        )

    kv_other_copy(0).start()
    for k in (1, 2, 3):
        kv_mine_copy(k).start()
        dev = across[k - 1]

        @pl.when(dev != device)
        def _():
            kv_other_copy(k).start()

        @pl.when(dev == device)
        def _():
            pltpu.make_async_copy(
                kv_other,
                kv.at[pl.ds((3 - k) * PAIR + BLK, BLK)],
                kv_recv_sem.at[2 * k + 1],
            ).start()

    loads[2].wait()
    for h in range(HEADS):
        lanes = slice(h * D, (h + 1) * D)
        mine, other = choose(q_in[:BLK, lanes], q_in[BLK:, lanes])
        q_all[h * BLK : (h + 1) * BLK] = mine
        q_other[h * BLK : (h + 1) * BLK] = other
    loads[3].wait()
    for h in range(HEADS):
        lanes = slice(h * D, (h + 1) * D)
        mine, other = choose(do_in[:BLK, lanes], do_in[BLK:, lanes])
        do_all[h * BLK : (h + 1) * BLK] = mine
        do_other[h * BLK : (h + 1) * BLK] = other

    def to_sibling(src, dst, index):
        return pltpu.make_async_remote_copy(
            src_ref=src,
            dst_ref=dst,
            send_sem=sib_send_sem.at[index],
            recv_sem=sib_recv_sem.at[index],
            device_id=coords(sibling),
            device_id_type=MESH,
        )

    q_move = to_sibling(q_other, q_all.at[pl.ds(COLS // 2, COLS // 2)], 0)
    do_move = to_sibling(do_other, do_all.at[pl.ds(COLS // 2, COLS // 2)], 1)
    q_move.start()
    do_move.start()

    loads[4].wait()
    key_iota = lax.broadcasted_iota(jnp.int32, (BLK, BLK), 0)
    query_iota = lax.broadcasted_iota(jnp.int32, (BLK, BLK), 1)

    def doc_row(window_block):
        block = 2 * worker - 6 + window_block
        return docs_in[jnp.maximum(block, 0) - first_row]

    query_docs = [jnp.broadcast_to(doc_row(6 + half), (BLK, BLK)) for half in (0, 1)]
    for block in range(8):
        key_docs = jnp.broadcast_to(doc_row(block).astype(F32), (BLK, BLK)).T.astype(jnp.int32)
        key_docs = jnp.where(2 * worker - 6 + block >= 0, key_docs, -1)
        for half in (0, 1):
            if block < half or block > 6 + half:
                continue
            allowed = key_docs == query_docs[half]
            if block == 6 + half:
                allowed = allowed & (key_iota <= query_iota)
            if block == half:
                allowed = allowed & (key_iota > query_iota)
            bias[half, block * BLK : (block + 1) * BLK] = jnp.where(allowed, 0.0, NEGATIVE)

    def scores(j, half):
        first, rows = rows_of(j, half)
        begin = j * PAIR + first

        def step(i, carry):
            t = half * 4 + i
            lanes = pl.ds(pl.multiple_of(t * PAIR, PAIR), PAIR)
            mask = bias[half, begin : begin + rows]
            s = dot_last(kv[begin : begin + rows, :D], q_all[lanes])
            s = s + jnp.concatenate([mask, mask], 1)
            g = dot_last(kv[begin : begin + rows, D:], do_all[lanes])
            top = jnp.max(s, axis=0, keepdims=True)
            e = jnp.exp2((s - top) * TO_EXP2)
            weights[j, t, first : first + rows] = e
            grad_prob[j, t, first : first + rows] = g
            st_max[j, t] = jnp.broadcast_to(top, (8, PAIR))
            st_sum[j, t] = jnp.sum(e.reshape(rows // 8, 8, PAIR), axis=0)
            st_dot[j, t] = jnp.sum((e * g).reshape(rows // 8, 8, PAIR), axis=0)
            return carry

        lax.fori_loop(0, 4, step, 0)

    def transpose_keys(j, first, rows):
        begin = j * PAIR + first
        key_t[:, begin : begin + rows] = kv[begin : begin + rows, :D].astype(F32).T.astype(BF16)

    scores(3, 0)
    transpose_keys(3, 0, BLK)
    kv_other_copy(0).wait_recv()
    q_move.wait_recv()
    do_move.wait_recv()
    scores(3, 1)
    transpose_keys(3, BLK, BLK)
    for j in (2, 1, 0):
        k = 3 - j
        kv_mine_copy(k).wait_recv()
        kv_other_copy(k).wait_recv()
        scores(j, 0)
        scores(j, 1)
        transpose_keys(j, 0, PAIR)

    def finish_stats(t, carry):
        tops = [st_max[j, t] for j in range(4)]
        top = jnp.maximum(jnp.maximum(tops[0], tops[1]), jnp.maximum(tops[2], tops[3]))
        scales = [jnp.exp2((tops[j] - top) * TO_EXP2) for j in range(4)]
        total = sum(st_sum[j, t] * scales[j] for j in range(4))
        dotted = sum(st_dot[j, t] * scales[j] for j in range(4))
        inverse = 1.0 / jnp.sum(total, axis=0, keepdims=True)
        row = jnp.sum(dotted, axis=0, keepdims=True) * inverse
        for j in range(4):
            st_scale[j, t] = scales[j] * inverse
        st_row[t] = jnp.broadcast_to(row, (8, PAIR))
        return carry

    lax.fori_loop(0, 8, finish_stats, 0)

    def grads_of(j):
        for half in (0, 1):
            first, rows = rows_of(j, half)

            def step(i, carry):
                t = half * 4 + i
                lanes = pl.ds(pl.multiple_of(t * PAIR, PAIR), PAIR)
                tall = (rows // 8, 8, PAIR)
                p = weights[j, t, first : first + rows].reshape(tall) * st_scale[j, t][None]
                g = grad_prob[j, t, first : first + rows].reshape(tall) - st_row[t][None]
                ds = (p * g).reshape(rows, PAIR)
                probs[first : first + rows, lanes] = p.reshape(rows, PAIR).astype(BF16)
                grads[j * PAIR + first : j * PAIR + first + rows, lanes] = ds.astype(BF16)
                return carry

            lax.fori_loop(0, 4, step, 0)

    def key_value_grads(j):
        if j in (1, 2):
            parts = [(0, PAIR, 0, COLS)]
        elif j == 0:
            parts = [(0, BLK, 0, COLS // 2), (BLK, BLK, 0, COLS)]
        else:
            parts = [(0, BLK, 0, COLS), (BLK, BLK, COLS // 2, COLS // 2)]
        for first, rows, lane, lanes in parts:
            begin = j * PAIR + first
            gk = dot_mid(grads[begin : begin + rows, lane : lane + lanes], q_all[lane : lane + lanes])
            gv = dot_mid(probs[first : first + rows, lane : lane + lanes], do_all[lane : lane + lanes])
            if j < 3:
                g_send[2 - j, first : first + rows, :D] = gk.astype(BF16)
                g_send[2 - j, first : first + rows, D:] = gv.astype(BF16)
            elif first == 0:
                own_grad[:, :D] = gk
                own_grad[:, D:] = gv
            else:
                sib_send[:, :D] = gk
                sib_send[:, D:] = gv

    def g_mine_copy(k):
        return pltpu.make_async_remote_copy(
            src_ref=g_send.at[k - 1, pl.ds(0, BLK)],
            dst_ref=g_mine.at[k - 1],
            send_sem=g_send_sem.at[2 * k - 2],
            recv_sem=g_recv_sem.at[2 * k - 2],
            device_id=coords(before[k - 1]),
            device_id_type=MESH,
        )

    def g_other_copy(k):
        return pltpu.make_async_remote_copy(
            src_ref=g_send.at[k - 1, pl.ds(BLK, BLK)],
            dst_ref=g_other.at[k - 1],
            send_sem=g_send_sem.at[2 * k - 1],
            recv_sem=g_recv_sem.at[2 * k - 1],
            device_id=coords(across[k - 1]),
            device_id_type=MESH,
        )

    for j in (0, 1, 2):
        k = 3 - j
        grads_of(j)
        key_value_grads(j)
        g_mine_copy(k).start()
        dev = across[k - 1]

        @pl.when(dev != device)
        def _():
            g_other_copy(k).start()

        @pl.when(dev == device)
        def _():
            pltpu.make_async_copy(
                g_send.at[k - 1, pl.ds(BLK, BLK)], g_other.at[k - 1], g_recv_sem.at[2 * k - 1]
            ).start()

    grads_of(3)
    key_value_grads(3)
    sib_move = to_sibling(sib_send, sib_recv, 2)
    sib_move.start()

    def query_grads(half, target):
        begin = half * BLK

        def step(i, carry):
            lanes = pl.ds(pl.multiple_of((half * 4 + i) * PAIR, PAIR), PAIR)
            g = dot_mid(key_t[:, begin : begin + 7 * BLK], grads[begin : begin + 7 * BLK, lanes])
            g = g * FACTOR
            for side in (0, 1):
                head = pl.ds(pl.multiple_of((i * 2 + side) * D, D), D)
                target[:, head] = g[:, side * BLK : (side + 1) * BLK].T.astype(BF16)
            return carry

        lax.fori_loop(0, 4, step, 0)

    query_grads(1, dq_send)
    dq_move = to_sibling(dq_send, dq_recv, 3)
    dq_move.start()
    query_grads(0, dq_mine)

    sib_move.wait_recv()
    dq_move.wait_recv()
    for h in range(HEADS):
        lanes = slice(h * D, (h + 1) * D)
        one, two = choose(dq_mine[:, lanes], dq_recv[:, lanes])
        dq_ref[:BLK, lanes] = one
        dq_ref[BLK:, lanes] = two

    mine_sum = own_grad[...]
    other_sum = sib_recv[...]
    for k in (3, 2, 1):
        g_mine_copy(k).wait_recv()
        g_other_copy(k).wait_recv()
        mine_sum = mine_sum + g_mine[k - 1].astype(F32)
        other_sum = other_sum + g_other[k - 1].astype(F32)
    one, two = choose(mine_sum, other_sum)
    dk_ref[:BLK] = (one[:, :D] * FACTOR).astype(BF16)
    dk_ref[BLK:] = (two[:, :D] * FACTOR).astype(BF16)
    dv_ref[:BLK] = one[:, D:].astype(BF16)
    dv_ref[BLK:] = two[:, D:].astype(BF16)

    kv_other_copy(0).wait_send()
    q_move.wait_send()
    do_move.wait_send()
    sib_move.wait_send()
    dq_move.wait_send()
    for k in (1, 2, 3):
        kv_mine_copy(k).wait_send()
        g_mine_copy(k).wait_send()

        @pl.when(across[k - 1] != device)
        def _():
            kv_other_copy(k).wait_send()
            g_other_copy(k).wait_send()


def on_device(queries, key_states, value_states, grad_output, documents, block_order):
    inner = lax.axis_size("inner")
    count = lax.axis_size("outer") * inner
    vmem = pl.BlockSpec(memory_space=pltpu.VMEM)
    hbm = pl.BlockSpec(memory_space=pl.ANY)
    docs = documents.reshape(2 * count, 1, BLK)
    return pl.pallas_call(
        functools.partial(kernel, count, inner),
        out_shape=[
            jax.ShapeDtypeStruct((PAIR, WIDE), BF16),
            jax.ShapeDtypeStruct((PAIR, D), BF16),
            jax.ShapeDtypeStruct((PAIR, D), BF16),
        ],
        in_specs=[pl.BlockSpec(memory_space=pltpu.SMEM)] + [hbm] * 5,
        out_specs=[vmem] * 3,
        scratch_shapes=[
            pltpu.VMEM((PAIR, WIDE), BF16),
            pltpu.VMEM((PAIR, WIDE), BF16),
            pltpu.VMEM((PAIR, D), BF16),
            pltpu.VMEM((PAIR, D), BF16),
            pltpu.VMEM((8, 1, BLK), jnp.int32),
            pltpu.VMEM((COLS, D), BF16),
            pltpu.VMEM((COLS, D), BF16),
            pltpu.VMEM((COLS // 2, D), BF16),
            pltpu.VMEM((COLS // 2, D), BF16),
            pltpu.VMEM((4 * PAIR, 2 * D), BF16),
            pltpu.VMEM((BLK, 2 * D), BF16),
            pltpu.VMEM((2, 4 * PAIR, BLK), F32),
            pltpu.VMEM((4, 8, PAIR, PAIR), F32),
            pltpu.VMEM((4, 8, PAIR, PAIR), F32),
            pltpu.VMEM((4, 8, 8, PAIR), F32),
            pltpu.VMEM((4, 8, 8, PAIR), F32),
            pltpu.VMEM((4, 8, 8, PAIR), F32),
            pltpu.VMEM((4, 8, 8, PAIR), F32),
            pltpu.VMEM((8, 8, PAIR), F32),
            pltpu.VMEM((PAIR, COLS), BF16),
            pltpu.VMEM((4 * PAIR, COLS), BF16),
            pltpu.VMEM((D, 4 * PAIR), BF16),
            pltpu.VMEM((3, PAIR, 2 * D), BF16),
            pltpu.VMEM((3, BLK, 2 * D), BF16),
            pltpu.VMEM((3, BLK, 2 * D), BF16),
            pltpu.VMEM((BLK, 2 * D), F32),
            pltpu.VMEM((BLK, 2 * D), F32),
            pltpu.VMEM((BLK, 2 * D), F32),
            pltpu.VMEM((BLK, WIDE), BF16),
            pltpu.VMEM((BLK, WIDE), BF16),
            pltpu.VMEM((BLK, WIDE), BF16),
            pltpu.SemaphoreType.DMA((5,)),
            pltpu.SemaphoreType.DMA((8,)),
            pltpu.SemaphoreType.DMA((8,)),
            pltpu.SemaphoreType.DMA((4,)),
            pltpu.SemaphoreType.DMA((4,)),
            pltpu.SemaphoreType.DMA((6,)),
            pltpu.SemaphoreType.DMA((6,)),
        ],
        compiler_params=pltpu.CompilerParams(
            collective_id=0, has_side_effects=True, vmem_limit_bytes=48 * 1024 * 1024
        ),
        name="attention_backward",
    )(block_order, docs, queries, key_states, value_states, grad_output)


def solution(mesh):
    rows = P(("outer", "inner"), None)
    return jax.shard_map(
        on_device,
        mesh=mesh,
        in_specs=(rows, rows, rows, rows, P(), P()),
        out_specs=(rows, rows, rows),
        check_vma=False,
    )
```

```python
import functools
import math

import jax
import jax.numpy as jnp
from jax import lax
from jax.experimental import pallas as pl
from jax.experimental.pallas import tpu as pltpu
from jax.sharding import PartitionSpec as P

BLK = 128
PAIR = 2 * BLK
D = 128
HEADS = 8
WIDE = HEADS * D
COLS = 2 * HEADS * BLK
NEGATIVE = -1e30
FACTOR = 1.0 / math.sqrt(D)
TO_EXP2 = FACTOR * math.log2(math.e)
MESH = pl.DeviceIdType.MESH
F32 = jnp.float32
BF16 = jnp.bfloat16
SCORE_UNROLL = 4
GRAD_UNROLL = 4
QUERY_UNROLL = 4


def dot_last(a, b):
    return lax.dot_general(a, b, (((1,), (1,)), ((), ())), preferred_element_type=F32)


def dot_mid(a, b):
    return lax.dot_general(a, b, (((1,), (0,)), ((), ())), preferred_element_type=F32)


def rows_of(j, half):
    if j == 0 and half == 1:
        return BLK, BLK
    if j == 3 and half == 0:
        return 0, BLK
    return 0, PAIR


def position(count, inner):
    device = lax.axis_index("outer") * inner + lax.axis_index("inner")
    core = lax.rem(device, 2)
    worker = lax.div(device, 2) + core * (count - 1 - 2 * lax.div(device, 2))
    return device, core, worker


def keeps_first(order_ref, device, core, count):
    low_first = (order_ref[2 * device] < count).astype(jnp.int32)
    return jnp.full((1, 1), low_first + core) == 1


def choose(flag, first, second):
    return jnp.where(flag, first, second), jnp.where(flag, second, first)


def main_kernel(
    count,
    inner,
    order_ref,
    docs_ref,
    q_ref,
    k_ref,
    v_ref,
    do_ref,
    dq_mine,
    dq_other,
    own_grad,
    sib_grad,
    g_mine,
    g_other,
    q_in,
    do_in,
    k_in,
    v_in,
    docs_in,
    q_all,
    do_all,
    q_other,
    do_other,
    kv,
    kv_other,
    bias,
    weights,
    grad_prob,
    st_max,
    st_sum,
    st_dot,
    st_scale,
    st_row,
    probs,
    grads,
    key_t,
    g_part,
    g_send,
    g_recv,
    own_keep,
    sib_send,
    dq_send,
    in_sem,
    kv_send_sem,
    kv_recv_sem,
    sib_send_sem,
    sib_recv_sem,
    g_send_sem,
    g_recv_sem,
    out_sem,
):
    device, core, worker = position(count, inner)
    mirror = count - 1 - worker

    def place(u):
        u = lax.rem(u + count, count)
        upper = lax.div(u, count // 2)
        return 2 * u + upper * (2 * count - 1 - 4 * u)

    def coords(dev):
        return (lax.div(dev, inner), lax.rem(dev, inner))

    after = place(worker + 1)
    before = place(worker - 1)
    across = place(mirror + 1)
    sibling = place(mirror)

    first_row = jnp.maximum(2 * worker - 6, 0)
    loads = [
        pltpu.make_async_copy(k_ref, k_in, in_sem.at[0]),
        pltpu.make_async_copy(v_ref, v_in, in_sem.at[1]),
        pltpu.make_async_copy(q_ref, q_in, in_sem.at[2]),
        pltpu.make_async_copy(do_ref, do_in, in_sem.at[3]),
        pltpu.make_async_copy(docs_ref.at[pl.ds(first_row, 8)], docs_in, in_sem.at[4]),
    ]
    for load in loads:
        load.start()

    barrier = pltpu.get_barrier_semaphore()
    for dev in (after, before, sibling):
        pl.semaphore_signal(barrier, inc=1, device_id=coords(dev), device_id_type=MESH)

    @pl.when(across != device)
    def _():
        pl.semaphore_signal(barrier, inc=1, device_id=coords(across), device_id_type=MESH)

    flag = keeps_first(order_ref, device, core, count)
    loads[0].wait()
    loads[1].wait()
    for lanes, ref in ((slice(0, D), k_in), (slice(D, 2 * D), v_in)):
        mine, other = choose(flag, ref[:BLK], ref[BLK:])
        kv[3 * PAIR : 3 * PAIR + BLK, lanes] = mine
        kv_other[:, lanes] = other

    pl.semaphore_wait(barrier, 4 - (across == device).astype(jnp.int32))

    def remote(src, dst, send_sem, recv_sem, dev):
        return pltpu.make_async_remote_copy(
            src_ref=src,
            dst_ref=dst,
            send_sem=send_sem,
            recv_sem=recv_sem,
            device_id=coords(dev),
            device_id_type=MESH,
        )

    def block_rows(k, half):
        return kv.at[pl.ds((3 - k) * PAIR + half * BLK, BLK)]

    def kv_copy(k, half):
        if half and k == 1:
            src, dev = kv_other, across
        else:
            src, dev = block_rows(k - 1, half), after
        index = 2 * k + half
        return remote(src, block_rows(k, half), kv_send_sem.at[index], kv_recv_sem.at[index], dev)

    def to_sibling(src, dst, index):
        return remote(src, dst, sib_send_sem.at[index], sib_recv_sem.at[index], sibling)

    kv_copy(1, 0).start()

    @pl.when(across != device)
    def _():
        kv_copy(1, 1).start()

    @pl.when(across == device)
    def _():
        pltpu.make_async_copy(kv_other, block_rows(1, 1), kv_recv_sem.at[3]).start()

    kv_move = to_sibling(kv_other, block_rows(0, 1), 4)
    kv_move.start()

    loads[2].wait()
    loads[3].wait()
    for h in range(HEADS):
        lanes = slice(h * D, (h + 1) * D)
        rows = slice(h * BLK, (h + 1) * BLK)
        q_all[rows], q_other[rows] = choose(flag, q_in[:BLK, lanes], q_in[BLK:, lanes])
        do_all[rows], do_other[rows] = choose(flag, do_in[:BLK, lanes], do_in[BLK:, lanes])
    q_move = to_sibling(q_other, q_all.at[pl.ds(COLS // 2, COLS // 2)], 0)
    do_move = to_sibling(do_other, do_all.at[pl.ds(COLS // 2, COLS // 2)], 1)
    q_move.start()
    do_move.start()

    loads[4].wait()
    key_iota = lax.broadcasted_iota(jnp.int32, (BLK, BLK), 0)
    query_iota = lax.broadcasted_iota(jnp.int32, (BLK, BLK), 1)

    def doc_row(window_block):
        block = 2 * worker - 6 + window_block
        return docs_in[jnp.maximum(block, 0) - first_row]

    def make_masks(blocks):
        query_docs = [jnp.broadcast_to(doc_row(6 + half), (BLK, BLK)) for half in (0, 1)]
        for block in blocks:
            key_docs = jnp.broadcast_to(doc_row(block).astype(F32), (BLK, BLK)).T.astype(jnp.int32)
            key_docs = jnp.where(2 * worker - 6 + block >= 0, key_docs, -1)
            for half in (0, 1):
                if block < half or block > 6 + half:
                    continue
                allowed = key_docs == query_docs[half]
                if block == 6 + half:
                    allowed = allowed & (key_iota <= query_iota)
                if block == half:
                    allowed = allowed & (key_iota > query_iota)
                bias[half, block * BLK : (block + 1) * BLK] = jnp.where(allowed, 0.0, NEGATIVE)

    def scores(j, half):
        first, rows = rows_of(j, half)
        begin = j * PAIR + first

        def step(i, carry):
            t = half * 4 + i
            lanes = pl.ds(pl.multiple_of(t * PAIR, PAIR), PAIR)
            mask = bias[half, begin : begin + rows]
            s = dot_last(kv[begin : begin + rows, :D], q_all[lanes])
            s = s + jnp.concatenate([mask, mask], 1)
            g = dot_last(kv[begin : begin + rows, D:], do_all[lanes])
            top = jnp.max(s, axis=0, keepdims=True)
            e = jnp.exp2((s - top) * TO_EXP2)
            weights[j, t, first : first + rows] = e
            grad_prob[j, t, first : first + rows] = g
            st_max[j, t] = jnp.broadcast_to(top, (8, PAIR))
            st_sum[j, t] = jnp.sum(e.reshape(rows // 8, 8, PAIR), axis=0)
            st_dot[j, t] = jnp.sum((e * g).reshape(rows // 8, 8, PAIR), axis=0)
            return carry

        lax.fori_loop(0, 4, step, 0, unroll=SCORE_UNROLL)

    def transpose_keys(j):
        begin = j * PAIR
        key_t[:, begin : begin + PAIR] = kv[begin : begin + PAIR, :D].astype(F32).T.astype(BF16)

    def pass_on(k):
        for half in (0, 1):
            kv_copy(k, half).wait_recv()
            kv_copy(k + 1, half).start()

    make_masks((6, 7))
    scores(3, 0)
    kv_move.wait_recv()
    make_masks((4, 5))
    pass_on(1)
    transpose_keys(3)
    q_move.wait_recv()
    do_move.wait_recv()
    scores(3, 1)
    scores(2, 0)
    pass_on(2)
    make_masks((0, 1, 2, 3))
    scores(2, 1)
    transpose_keys(2)
    scores(1, 0)
    scores(1, 1)
    transpose_keys(1)
    kv_copy(3, 0).wait_recv()
    kv_copy(3, 1).wait_recv()
    scores(0, 0)
    scores(0, 1)

    def finish_stats(t, carry):
        tops = [st_max[j, t] for j in range(4)]
        top = jnp.maximum(jnp.maximum(tops[0], tops[1]), jnp.maximum(tops[2], tops[3]))
        scales = [jnp.exp2((tops[j] - top) * TO_EXP2) for j in range(4)]
        total = sum(st_sum[j, t] * scales[j] for j in range(4))
        dotted = sum(st_dot[j, t] * scales[j] for j in range(4))
        inverse = 1.0 / jnp.sum(total, axis=0, keepdims=True)
        row = jnp.sum(dotted, axis=0, keepdims=True) * inverse
        for j in range(4):
            st_scale[j, t] = scales[j] * inverse
        st_row[t] = jnp.broadcast_to(row, (8, PAIR))
        return carry

    lax.fori_loop(0, 8, finish_stats, 0, unroll=4)

    def grads_of(j):
        for half in (0, 1):
            first, rows = rows_of(j, half)

            def step(i, carry):
                t = half * 4 + i
                lanes = pl.ds(pl.multiple_of(t * PAIR, PAIR), PAIR)
                tall = (rows // 8, 8, PAIR)
                p = weights[j, t, first : first + rows].reshape(tall) * st_scale[j, t][None]
                g = grad_prob[j, t, first : first + rows].reshape(tall) - st_row[t][None]
                ds = (p * g).reshape(rows, PAIR)
                probs[first : first + rows, lanes] = p.reshape(rows, PAIR).astype(BF16)
                grads[j * PAIR + first : j * PAIR + first + rows, lanes] = ds.astype(BF16)
                return carry

            lax.fori_loop(0, 4, step, 0, unroll=GRAD_UNROLL)

    def key_value_grads(j, half):
        lane, lanes = 0, COLS
        if j == 0 and half == 0:
            lanes = COLS // 2
        if j == 3 and half == 1:
            lane, lanes = COLS // 2, COLS // 2
        first = half * BLK
        begin = j * PAIR + first
        gk = dot_mid(grads[begin : begin + BLK, lane : lane + lanes], q_all[lane : lane + lanes])
        gv = dot_mid(probs[first : first + BLK, lane : lane + lanes], do_all[lane : lane + lanes])
        return gk, gv

    def g_copy(k, half):
        if k > 1:
            dst, dev = g_recv.at[k - 2, half], before
        else:
            dst, dev = (g_other, across) if half else (g_mine, before)
        index = 2 * (k - 1) + half
        return remote(g_send.at[k - 1, half], dst, g_send_sem.at[index], g_recv_sem.at[index], dev)

    grads_of(0)
    for half in (0, 1):
        gk, gv = key_value_grads(0, half)
        g_send[2, half, :, :D] = gk.astype(BF16)
        g_send[2, half, :, D:] = gv.astype(BF16)
        g_copy(3, half).start()

    def part_of(k):
        grads_of(3 - k)
        for half in (0, 1):
            gk, gv = key_value_grads(3 - k, half)
            g_part[k - 1, half, :, :D] = gk
            g_part[k - 1, half, :, D:] = gv

    def add_and_send(k):
        for half in (0, 1):
            g_copy(k + 1, half).wait_recv()
            total = g_part[k - 1, half] + g_recv[k - 1, half].astype(F32)
            g_send[k - 1, half] = total.astype(BF16)
            if k == 1 and half == 1:

                @pl.when(across != device)
                def _():
                    g_copy(1, 1).start()

                @pl.when(across == device)
                def _():
                    pltpu.make_async_copy(g_send.at[0, 1], g_other, g_recv_sem.at[1]).start()
            else:
                g_copy(k, half).start()

    def query_grads(half, emit):
        begin = half * BLK

        def step(i, carry):
            lanes = pl.ds(pl.multiple_of((half * 4 + i) * PAIR, PAIR), PAIR)
            g = dot_mid(key_t[:, begin : begin + 7 * BLK], grads[begin : begin + 7 * BLK, lanes])
            g = g * FACTOR
            for side in (0, 1):
                head = pl.ds(pl.multiple_of((i * 2 + side) * D, D), D)
                dq_send[half, :, head] = g[:, side * BLK : (side + 1) * BLK].T.astype(BF16)
            return carry

        lax.fori_loop(0, 4, step, 0, unroll=QUERY_UNROLL)

    part_of(2)
    part_of(1)
    add_and_send(2)
    transpose_keys(0)
    grads_of(3)
    gk, gv = key_value_grads(3, 1)
    sib_send[:, :D] = gk
    sib_send[:, D:] = gv
    sib_move = to_sibling(sib_send, sib_grad, 2)
    sib_move.start()
    gk, gv = key_value_grads(3, 0)
    own_keep[:, :D] = gk
    own_keep[:, D:] = gv
    own_out = pltpu.make_async_copy(own_keep, own_grad, out_sem.at[0])
    own_out.start()
    query_grads(1, None)
    dq_move = to_sibling(dq_send.at[1], dq_other, 3)
    dq_move.start()
    add_and_send(1)
    query_grads(0, None)
    dq_out = pltpu.make_async_copy(dq_send.at[0], dq_mine, out_sem.at[1])
    dq_out.start()

    own_out.wait()
    for move in (q_move, do_move, kv_move, sib_move, dq_move):
        move.wait_send()
    for k in (1, 2, 3):
        for half in (0, 1):
            if k == 1 and half == 1:

                @pl.when(across != device)
                def _():
                    kv_copy(1, 1).wait_send()
                    g_copy(1, 1).wait_send()
            else:
                kv_copy(k, half).wait_send()
                g_copy(k, half).wait_send()
    sib_move.wait_recv()
    dq_out.wait()
    dq_move.wait_recv()
    g_copy(1, 0).wait_recv()
    g_copy(1, 1).wait_recv()


def last_kernel(
    count,
    inner,
    order_ref,
    dq_mine,
    dq_other,
    own_grad,
    sib_grad,
    g_mine,
    g_other,
    dq_ref,
    dk_ref,
    dv_ref,
):
    device, core, _ = position(count, inner)
    flag = keeps_first(order_ref, device, core, count)
    dq_ref[:BLK], dq_ref[BLK:] = choose(flag, dq_mine[...], dq_other[...])
    mine = own_grad[...] + g_mine[...].astype(F32)
    other = sib_grad[...] + g_other[...].astype(F32)
    one, two = choose(flag, mine, other)
    dk_ref[:BLK] = (one[:, :D] * FACTOR).astype(BF16)
    dk_ref[BLK:] = (two[:, :D] * FACTOR).astype(BF16)
    dv_ref[:BLK] = one[:, D:].astype(BF16)
    dv_ref[BLK:] = two[:, D:].astype(BF16)


def on_device(queries, key_states, value_states, grad_output, documents, block_order):
    inner = lax.axis_size("inner")
    count = lax.axis_size("outer") * inner
    smem = pl.BlockSpec(memory_space=pltpu.SMEM)
    vmem = pl.BlockSpec(memory_space=pltpu.VMEM)
    hbm = pl.BlockSpec(memory_space=pl.ANY)
    docs = documents.reshape(2 * count, 1, BLK)
    mid = pl.pallas_call(
        functools.partial(main_kernel, count, inner),
        out_shape=[
            jax.ShapeDtypeStruct((BLK, WIDE), BF16),
            jax.ShapeDtypeStruct((BLK, WIDE), BF16),
            jax.ShapeDtypeStruct((BLK, 2 * D), F32),
            jax.ShapeDtypeStruct((BLK, 2 * D), F32),
            jax.ShapeDtypeStruct((BLK, 2 * D), BF16),
            jax.ShapeDtypeStruct((BLK, 2 * D), BF16),
        ],
        in_specs=[smem] + [hbm] * 5,
        out_specs=[hbm] * 6,
        scratch_shapes=[
            pltpu.VMEM((PAIR, WIDE), BF16),
            pltpu.VMEM((PAIR, WIDE), BF16),
            pltpu.VMEM((PAIR, D), BF16),
            pltpu.VMEM((PAIR, D), BF16),
            pltpu.VMEM((8, 1, BLK), jnp.int32),
            pltpu.VMEM((COLS, D), BF16),
            pltpu.VMEM((COLS, D), BF16),
            pltpu.VMEM((COLS // 2, D), BF16),
            pltpu.VMEM((COLS // 2, D), BF16),
            pltpu.VMEM((4 * PAIR, 2 * D), BF16),
            pltpu.VMEM((BLK, 2 * D), BF16),
            pltpu.VMEM((2, 4 * PAIR, BLK), F32),
            pltpu.VMEM((4, 8, PAIR, PAIR), F32),
            pltpu.VMEM((4, 8, PAIR, PAIR), F32),
            pltpu.VMEM((4, 8, 8, PAIR), F32),
            pltpu.VMEM((4, 8, 8, PAIR), F32),
            pltpu.VMEM((4, 8, 8, PAIR), F32),
            pltpu.VMEM((4, 8, 8, PAIR), F32),
            pltpu.VMEM((8, 8, PAIR), F32),
            pltpu.VMEM((PAIR, COLS), BF16),
            pltpu.VMEM((4 * PAIR, COLS), BF16),
            pltpu.VMEM((D, 4 * PAIR), BF16),
            pltpu.VMEM((2, 2, BLK, 2 * D), F32),
            pltpu.VMEM((3, 2, BLK, 2 * D), BF16),
            pltpu.VMEM((2, 2, BLK, 2 * D), BF16),
            pltpu.VMEM((BLK, 2 * D), F32),
            pltpu.VMEM((BLK, 2 * D), F32),
            pltpu.VMEM((2, BLK, WIDE), BF16),
            pltpu.SemaphoreType.DMA((5,)),
            pltpu.SemaphoreType.DMA((8,)),
            pltpu.SemaphoreType.DMA((8,)),
            pltpu.SemaphoreType.DMA((5,)),
            pltpu.SemaphoreType.DMA((5,)),
            pltpu.SemaphoreType.DMA((6,)),
            pltpu.SemaphoreType.DMA((6,)),
            pltpu.SemaphoreType.DMA((2,)),
        ],
        compiler_params=pltpu.CompilerParams(
            collective_id=0, has_side_effects=True, vmem_limit_bytes=60 * 1024 * 1024
        ),
        name="attention_backward",
    )(block_order, docs, queries, key_states, value_states, grad_output)
    return pl.pallas_call(
        functools.partial(last_kernel, count, inner),
        out_shape=[
            jax.ShapeDtypeStruct((PAIR, WIDE), BF16),
            jax.ShapeDtypeStruct((PAIR, D), BF16),
            jax.ShapeDtypeStruct((PAIR, D), BF16),
        ],
        in_specs=[smem] + [vmem] * 6,
        out_specs=[vmem] * 3,
        name="stored_order",
    )(block_order, *mid)


def solution(mesh):
    rows = P(("outer", "inner"), None)
    return jax.shard_map(
        on_device,
        mesh=mesh,
        in_specs=(rows, rows, rows, rows, P(), P()),
        out_specs=(rows, rows, rows),
        check_vma=False,
    )
```

```python
import functools
import math

import jax
import jax.numpy as jnp
from jax import lax
from jax.experimental import pallas as pl
from jax.experimental.pallas import tpu as pltpu
from jax.sharding import PartitionSpec as P

BLK = 128
PAIR = 2 * BLK
D = 128
HEADS = 8
WIDE = HEADS * D
COLS = 2 * HEADS * BLK
NEGATIVE = -1e30
FACTOR = 1.0 / math.sqrt(D)
TO_EXP2 = FACTOR * math.log2(math.e)
MESH = pl.DeviceIdType.MESH
F32 = jnp.float32
BF16 = jnp.bfloat16
SCORE_UNROLL = 4
GRAD_UNROLL = 4
QUERY_UNROLL = 4
PIECES = 2
PIECE = BLK // PIECES


def dot_last(a, b):
    return lax.dot_general(a, b, (((1,), (1,)), ((), ())), preferred_element_type=F32)


def dot_mid(a, b):
    return lax.dot_general(a, b, (((1,), (0,)), ((), ())), preferred_element_type=F32)


def rows_of(j, half):
    if j == 0 and half == 1:
        return BLK, BLK
    if j == 3 and half == 0:
        return 0, BLK
    return 0, PAIR


def position(count, inner):
    device = lax.axis_index("outer") * inner + lax.axis_index("inner")
    core = lax.rem(device, 2)
    worker = lax.div(device, 2) + core * (count - 1 - 2 * lax.div(device, 2))
    return device, core, worker


def order_row(order_ref, order_in, device, sem):
    return pltpu.make_async_copy(order_ref.at[lax.div(2 * device, BLK)], order_in, sem)


def keeps_first(order_in, device, core, count):
    low_first = (order_in[0, lax.rem(2 * device, BLK)] < count).astype(jnp.int32)
    return low_first + core


def choose(flag, first, second):
    return jnp.where(flag, first, second), jnp.where(flag, second, first)


def main_kernel(
    count,
    inner,
    order_ref,
    docs_ref,
    q_ref,
    k_ref,
    v_ref,
    do_ref,
    dq_mine,
    dq_other,
    own_grad,
    sib_grad,
    g_mine,
    g_other,
    q_in,
    do_in,
    k_in,
    v_in,
    docs_in,
    q_all,
    do_all,
    q_other,
    do_other,
    kv,
    kv_other,
    bias,
    weights,
    grad_prob,
    st_max,
    st_sum,
    st_dot,
    st_scale,
    st_row,
    probs,
    grads,
    key_t,
    g_part,
    g_send,
    g_recv,
    own_keep,
    sib_send,
    dq_send,
    order_in,
    in_sem,
    kv_send_sem,
    kv_recv_sem,
    sib_send_sem,
    sib_recv_sem,
    g_send_sem,
    g_recv_sem,
    out_sem,
):
    device, core, worker = position(count, inner)
    mirror = count - 1 - worker

    def place(u):
        u = lax.rem(u + count, count)
        upper = lax.div(u, count // 2)
        return 2 * u + upper * (2 * count - 1 - 4 * u)

    def coords(dev):
        return (lax.div(dev, inner), lax.rem(dev, inner))

    after = place(worker + 1)
    before = place(worker - 1)
    across = place(mirror + 1)
    sibling = place(mirror)

    first_row = jnp.maximum(2 * worker - 6, 0)
    loads = [
        pltpu.make_async_copy(k_ref, k_in, in_sem.at[0]),
        pltpu.make_async_copy(v_ref, v_in, in_sem.at[1]),
        pltpu.make_async_copy(q_ref, q_in, in_sem.at[2]),
        pltpu.make_async_copy(do_ref, do_in, in_sem.at[3]),
        pltpu.make_async_copy(docs_ref.at[pl.ds(first_row, 8)], docs_in, in_sem.at[4]),
        order_row(order_ref, order_in, device, in_sem.at[5]),
    ]
    for load in (loads[0], loads[1], loads[5], loads[2], loads[3], loads[4]):
        load.start()

    barrier = pltpu.get_barrier_semaphore()
    for dev in (before, sibling):
        pl.semaphore_signal(barrier, inc=1, device_id=coords(dev), device_id_type=MESH)

    @pl.when(across != device)
    def _():
        pl.semaphore_signal(barrier, inc=1, device_id=coords(across), device_id_type=MESH)

    loads[5].wait()
    flag = jnp.full((1, 1), keeps_first(order_in, device, core, count)) == 1
    loads[0].wait()
    loads[1].wait()
    for lanes, ref in ((slice(0, D), k_in), (slice(D, 2 * D), v_in)):
        mine, other = choose(flag, ref[:BLK], ref[BLK:])
        kv[3 * PAIR : 3 * PAIR + BLK, lanes] = mine
        kv_other[:, lanes] = other

    pl.semaphore_wait(barrier, 3 - (across == device).astype(jnp.int32))

    def remote(src, dst, send_sem, recv_sem, dev):
        return pltpu.make_async_remote_copy(
            src_ref=src,
            dst_ref=dst,
            send_sem=send_sem,
            recv_sem=recv_sem,
            device_id=coords(dev),
            device_id_type=MESH,
        )

    def piece_rows(k, half, piece):
        return kv.at[pl.ds((3 - k) * PAIR + half * BLK + piece * PIECE, PIECE)]

    def kv_copy(k, half, piece):
        if half and k == 1:
            src, dev = kv_other.at[pl.ds(piece * PIECE, PIECE)], across
        else:
            src, dev = piece_rows(k - 1, half, piece), after
        sems = kv_send_sem.at[k - 1, half, piece], kv_recv_sem.at[k - 1, half, piece]
        return remote(src, piece_rows(k, half, piece), *sems, dev)

    def to_sibling(src, dst, index):
        return remote(src, dst, sib_send_sem.at[index], sib_recv_sem.at[index], sibling)

    for piece in range(PIECES):
        kv_copy(1, 0, piece).start()

    @pl.when(across != device)
    def _():
        for piece in range(PIECES):
            kv_copy(1, 1, piece).start()

    @pl.when(across == device)
    def _():
        for piece in range(PIECES):
            pltpu.make_async_copy(
                kv_other.at[pl.ds(piece * PIECE, PIECE)],
                piece_rows(1, 1, piece),
                kv_recv_sem.at[0, 1, piece],
            ).start()

    kv_move = to_sibling(kv_other, kv.at[pl.ds(3 * PAIR + BLK, BLK)], 4)
    kv_move.start()

    loads[2].wait()
    loads[3].wait()
    for h in range(HEADS):
        lanes = slice(h * D, (h + 1) * D)
        rows = slice(h * BLK, (h + 1) * BLK)
        q_all[rows], q_other[rows] = choose(flag, q_in[:BLK, lanes], q_in[BLK:, lanes])
        do_all[rows], do_other[rows] = choose(flag, do_in[:BLK, lanes], do_in[BLK:, lanes])
    q_move = to_sibling(q_other, q_all.at[pl.ds(COLS // 2, COLS // 2)], 0)
    do_move = to_sibling(do_other, do_all.at[pl.ds(COLS // 2, COLS // 2)], 1)
    q_move.start()
    do_move.start()

    loads[4].wait()
    key_iota = lax.broadcasted_iota(jnp.int32, (BLK, BLK), 0)
    query_iota = lax.broadcasted_iota(jnp.int32, (BLK, BLK), 1)

    def doc_row(window_block):
        block = 2 * worker - 6 + window_block
        return docs_in[jnp.maximum(block, 0) - first_row]

    def make_masks(blocks):
        query_docs = [jnp.broadcast_to(doc_row(6 + half), (BLK, BLK)) for half in (0, 1)]
        for block in blocks:
            key_docs = jnp.broadcast_to(doc_row(block).astype(F32), (BLK, BLK)).T.astype(jnp.int32)
            key_docs = jnp.where(2 * worker - 6 + block >= 0, key_docs, -1)
            for half in (0, 1):
                if block < half or block > 6 + half:
                    continue
                allowed = key_docs == query_docs[half]
                if block == 6 + half:
                    allowed = allowed & (key_iota <= query_iota)
                if block == half:
                    allowed = allowed & (key_iota > query_iota)
                bias[half, block * BLK : (block + 1) * BLK] = jnp.where(allowed, 0.0, NEGATIVE)

    def scores(j, half):
        first, rows = rows_of(j, half)
        begin = j * PAIR + first

        def step(i, carry):
            t = half * 4 + i
            lanes = pl.ds(pl.multiple_of(t * PAIR, PAIR), PAIR)
            mask = bias[half, begin : begin + rows]
            s = dot_last(kv[begin : begin + rows, :D], q_all[lanes])
            s = s + jnp.concatenate([mask, mask], 1)
            g = dot_last(kv[begin : begin + rows, D:], do_all[lanes])
            top = jnp.max(s, axis=0, keepdims=True)
            e = jnp.exp2((s - top) * TO_EXP2)
            weights[j, t, first : first + rows] = e
            grad_prob[j, t, first : first + rows] = g
            st_max[j, t] = jnp.broadcast_to(top, (8, PAIR))
            st_sum[j, t] = jnp.sum(e.reshape(rows // 8, 8, PAIR), axis=0)
            st_dot[j, t] = jnp.sum((e * g).reshape(rows // 8, 8, PAIR), axis=0)
            return carry

        lax.fori_loop(0, 4, step, 0, unroll=SCORE_UNROLL)

    def transpose_keys(j):
        begin = j * PAIR
        key_t[:, begin : begin + PAIR] = kv[begin : begin + PAIR, :D].astype(F32).T.astype(BF16)

    def pass_on(k):
        for half in (0, 1):
            for piece in range(PIECES):
                kv_copy(k, half, piece).wait_recv()
                kv_copy(k + 1, half, piece).start()

    make_masks((6, 7))
    scores(3, 0)
    kv_move.wait_recv()
    make_masks((4, 5))
    pass_on(1)
    transpose_keys(3)
    q_move.wait_recv()
    do_move.wait_recv()
    scores(3, 1)
    scores(2, 0)
    pass_on(2)
    make_masks((0, 1, 2, 3))
    scores(2, 1)
    transpose_keys(2)
    scores(1, 0)
    scores(1, 1)
    transpose_keys(1)
    for half in (0, 1):
        for piece in range(PIECES):
            kv_copy(3, half, piece).wait_recv()
    scores(0, 0)
    scores(0, 1)

    def finish_stats(t, carry):
        tops = [st_max[j, t] for j in range(4)]
        top = jnp.maximum(jnp.maximum(tops[0], tops[1]), jnp.maximum(tops[2], tops[3]))
        scales = [jnp.exp2((tops[j] - top) * TO_EXP2) for j in range(4)]
        total = sum(st_sum[j, t] * scales[j] for j in range(4))
        dotted = sum(st_dot[j, t] * scales[j] for j in range(4))
        inverse = 1.0 / jnp.sum(total, axis=0, keepdims=True)
        row = jnp.sum(dotted, axis=0, keepdims=True) * inverse
        for j in range(4):
            st_scale[j, t] = scales[j] * inverse
        st_row[t] = jnp.broadcast_to(row, (8, PAIR))
        return carry

    lax.fori_loop(0, 8, finish_stats, 0, unroll=4)

    def grads_of(j):
        for half in (0, 1):
            first, rows = rows_of(j, half)

            def step(i, carry):
                t = half * 4 + i
                lanes = pl.ds(pl.multiple_of(t * PAIR, PAIR), PAIR)
                tall = (rows // 8, 8, PAIR)
                p = weights[j, t, first : first + rows].reshape(tall) * st_scale[j, t][None]
                g = grad_prob[j, t, first : first + rows].reshape(tall) - st_row[t][None]
                ds = (p * g).reshape(rows, PAIR)
                probs[first : first + rows, lanes] = p.reshape(rows, PAIR).astype(BF16)
                grads[j * PAIR + first : j * PAIR + first + rows, lanes] = ds.astype(BF16)
                return carry

            lax.fori_loop(0, 4, step, 0, unroll=GRAD_UNROLL)

    def key_value_grads(j, half):
        lane, lanes = 0, COLS
        if j == 0 and half == 0:
            lanes = COLS // 2
        if j == 3 and half == 1:
            lane, lanes = COLS // 2, COLS // 2
        first = half * BLK
        begin = j * PAIR + first
        gk = dot_mid(grads[begin : begin + BLK, lane : lane + lanes], q_all[lane : lane + lanes])
        gv = dot_mid(probs[first : first + BLK, lane : lane + lanes], do_all[lane : lane + lanes])
        return gk, gv

    def g_copy(k, half, piece):
        rows = pl.ds(piece * PIECE, PIECE)
        if k > 1:
            dst, dev = g_recv.at[k - 2, half, rows], before
        elif half:
            dst, dev = g_other.at[rows], across
        else:
            dst, dev = g_mine.at[rows], before
        sems = g_send_sem.at[k - 1, half, piece], g_recv_sem.at[k - 1, half, piece]
        return remote(g_send.at[k - 1, half, rows], dst, *sems, dev)

    grads_of(0)
    for half in (0, 1):
        gk, gv = key_value_grads(0, half)
        g_send[2, half, :, :D] = gk.astype(BF16)
        g_send[2, half, :, D:] = gv.astype(BF16)
        for piece in range(PIECES):
            g_copy(3, half, piece).start()

    def part_of(k):
        grads_of(3 - k)
        for half in (0, 1):
            gk, gv = key_value_grads(3 - k, half)
            g_part[k - 1, half, :, :D] = gk
            g_part[k - 1, half, :, D:] = gv

    def add_and_send(k):
        for half in (0, 1):
            for piece in range(PIECES):
                rows = pl.ds(piece * PIECE, PIECE)
                g_copy(k + 1, half, piece).wait_recv()
                total = g_part[k - 1, half, rows] + g_recv[k - 1, half, rows].astype(F32)
                g_send[k - 1, half, rows] = total.astype(BF16)
                if k == 1 and half == 1:

                    @pl.when(across != device)
                    def _():
                        g_copy(1, 1, piece).start()

                    @pl.when(across == device)
                    def _():
                        pltpu.make_async_copy(
                            g_send.at[0, 1, rows], g_other.at[rows], g_recv_sem.at[0, 1, piece]
                        ).start()
                else:
                    g_copy(k, half, piece).start()

    def query_grads(half, emit):
        begin = half * BLK

        def step(i, carry):
            lanes = pl.ds(pl.multiple_of((half * 4 + i) * PAIR, PAIR), PAIR)
            g = dot_mid(key_t[:, begin : begin + 7 * BLK], grads[begin : begin + 7 * BLK, lanes])
            g = g * FACTOR
            for side in (0, 1):
                head = pl.ds(pl.multiple_of((i * 2 + side) * D, D), D)
                dq_send[half, :, head] = g[:, side * BLK : (side + 1) * BLK].T.astype(BF16)
            return carry

        lax.fori_loop(0, 4, step, 0, unroll=QUERY_UNROLL)

    part_of(2)
    part_of(1)
    add_and_send(2)
    transpose_keys(0)
    grads_of(3)
    gk, gv = key_value_grads(3, 1)
    sib_send[:, :D] = gk
    sib_send[:, D:] = gv
    sib_move = to_sibling(sib_send, sib_grad, 2)
    sib_move.start()
    gk, gv = key_value_grads(3, 0)
    own_keep[:, :D] = gk
    own_keep[:, D:] = gv
    own_out = pltpu.make_async_copy(own_keep, own_grad, out_sem.at[0])
    own_out.start()
    query_grads(1, None)
    dq_move = to_sibling(dq_send.at[1], dq_other, 3)
    dq_move.start()
    add_and_send(1)
    query_grads(0, None)
    dq_out = pltpu.make_async_copy(dq_send.at[0], dq_mine, out_sem.at[1])
    dq_out.start()

    own_out.wait()
    for move in (q_move, do_move, kv_move, sib_move, dq_move):
        move.wait_send()
    for k in (1, 2, 3):
        for half in (0, 1):
            for piece in range(PIECES):
                if k == 1 and half == 1:

                    @pl.when(across != device)
                    def _():
                        kv_copy(1, 1, piece).wait_send()
                        g_copy(1, 1, piece).wait_send()
                else:
                    kv_copy(k, half, piece).wait_send()
                    g_copy(k, half, piece).wait_send()
    sib_move.wait_recv()
    dq_out.wait()
    dq_move.wait_recv()
    for half in (0, 1):
        for piece in range(PIECES):
            g_copy(1, half, piece).wait_recv()


def last_kernel(
    count,
    inner,
    order_ref,
    dq_mine,
    dq_other,
    own_grad,
    sib_grad,
    g_mine,
    g_other,
    dq_ref,
    dk_ref,
    dv_ref,
    dq_in,
    near_in,
    far_in,
    dk_out,
    dv_out,
    order_in,
    in_sem,
    out_sem,
):
    device, core, _ = position(count, inner)
    order = order_row(order_ref, order_in, device, in_sem.at[6])
    loads = [
        pltpu.make_async_copy(dq_mine, dq_in.at[0], in_sem.at[0]),
        pltpu.make_async_copy(dq_other, dq_in.at[1], in_sem.at[1]),
        pltpu.make_async_copy(own_grad, near_in.at[0], in_sem.at[2]),
        pltpu.make_async_copy(g_mine, far_in.at[0], in_sem.at[3]),
        pltpu.make_async_copy(sib_grad, near_in.at[1], in_sem.at[4]),
        pltpu.make_async_copy(g_other, far_in.at[1], in_sem.at[5]),
    ]
    order.start()
    for load in loads:
        load.start()
    order.wait()
    mine_slot = jnp.where(keeps_first(order_in, device, core, count) == 1, 0, 1)
    stores = []
    for which in (0, 1):
        slot = mine_slot if which == 0 else 1 - mine_slot
        rows = pl.ds(pl.multiple_of(slot * BLK, BLK), BLK)
        loads[which].wait()
        stores.append(pltpu.make_async_copy(dq_in.at[which], dq_ref.at[rows], out_sem.at[3 * which]))
        stores[-1].start()
    for which in (0, 1):
        slot = mine_slot if which == 0 else 1 - mine_slot
        rows = pl.ds(pl.multiple_of(slot * BLK, BLK), BLK)
        loads[2 + 2 * which].wait()
        loads[3 + 2 * which].wait()
        total = near_in[which] + far_in[which].astype(F32)
        dk_out[which] = (total[:, :D] * FACTOR).astype(BF16)
        dv_out[which] = total[:, D:].astype(BF16)
        for step, (src, dst) in enumerate(((dk_out, dk_ref), (dv_out, dv_ref))):
            sem = out_sem.at[3 * which + 1 + step]
            stores.append(pltpu.make_async_copy(src.at[which], dst.at[rows], sem))
            stores[-1].start()
    for store in stores:
        store.wait()


def on_device(queries, key_states, value_states, grad_output, documents, block_order):
    inner = lax.axis_size("inner")
    count = lax.axis_size("outer") * inner
    hbm = pl.BlockSpec(memory_space=pl.ANY)
    docs = documents.reshape(2 * count, 1, BLK)
    order = block_order.reshape(2 * count // BLK, 1, BLK)
    mid = pl.pallas_call(
        functools.partial(main_kernel, count, inner),
        out_shape=[
            jax.ShapeDtypeStruct((BLK, WIDE), BF16),
            jax.ShapeDtypeStruct((BLK, WIDE), BF16),
            jax.ShapeDtypeStruct((BLK, 2 * D), F32),
            jax.ShapeDtypeStruct((BLK, 2 * D), F32),
            jax.ShapeDtypeStruct((BLK, 2 * D), BF16),
            jax.ShapeDtypeStruct((BLK, 2 * D), BF16),
        ],
        in_specs=[hbm] * 6,
        out_specs=[hbm] * 6,
        scratch_shapes=[
            pltpu.VMEM((PAIR, WIDE), BF16),
            pltpu.VMEM((PAIR, WIDE), BF16),
            pltpu.VMEM((PAIR, D), BF16),
            pltpu.VMEM((PAIR, D), BF16),
            pltpu.VMEM((8, 1, BLK), jnp.int32),
            pltpu.VMEM((COLS, D), BF16),
            pltpu.VMEM((COLS, D), BF16),
            pltpu.VMEM((COLS // 2, D), BF16),
            pltpu.VMEM((COLS // 2, D), BF16),
            pltpu.VMEM((4 * PAIR, 2 * D), BF16),
            pltpu.VMEM((BLK, 2 * D), BF16),
            pltpu.VMEM((2, 4 * PAIR, BLK), F32),
            pltpu.VMEM((4, 8, PAIR, PAIR), F32),
            pltpu.VMEM((4, 8, PAIR, PAIR), F32),
            pltpu.VMEM((4, 8, 8, PAIR), F32),
            pltpu.VMEM((4, 8, 8, PAIR), F32),
            pltpu.VMEM((4, 8, 8, PAIR), F32),
            pltpu.VMEM((4, 8, 8, PAIR), F32),
            pltpu.VMEM((8, 8, PAIR), F32),
            pltpu.VMEM((PAIR, COLS), BF16),
            pltpu.VMEM((4 * PAIR, COLS), BF16),
            pltpu.VMEM((D, 4 * PAIR), BF16),
            pltpu.VMEM((2, 2, BLK, 2 * D), F32),
            pltpu.VMEM((3, 2, BLK, 2 * D), BF16),
            pltpu.VMEM((2, 2, BLK, 2 * D), BF16),
            pltpu.VMEM((BLK, 2 * D), F32),
            pltpu.VMEM((BLK, 2 * D), F32),
            pltpu.VMEM((2, BLK, WIDE), BF16),
            pltpu.SMEM((1, BLK), jnp.int32),
            pltpu.SemaphoreType.DMA((6,)),
            pltpu.SemaphoreType.DMA((3, 2, PIECES)),
            pltpu.SemaphoreType.DMA((3, 2, PIECES)),
            pltpu.SemaphoreType.DMA((5,)),
            pltpu.SemaphoreType.DMA((5,)),
            pltpu.SemaphoreType.DMA((3, 2, PIECES)),
            pltpu.SemaphoreType.DMA((3, 2, PIECES)),
            pltpu.SemaphoreType.DMA((2,)),
        ],
        compiler_params=pltpu.CompilerParams(
            collective_id=0, has_side_effects=True, vmem_limit_bytes=60 * 1024 * 1024
        ),
        name="attention_backward",
    )(order, docs, queries, key_states, value_states, grad_output)
    return pl.pallas_call(
        functools.partial(last_kernel, count, inner),
        out_shape=[
            jax.ShapeDtypeStruct((PAIR, WIDE), BF16),
            jax.ShapeDtypeStruct((PAIR, D), BF16),
            jax.ShapeDtypeStruct((PAIR, D), BF16),
        ],
        in_specs=[hbm] * 7,
        out_specs=[hbm] * 3,
        scratch_shapes=[
            pltpu.VMEM((2, BLK, WIDE), BF16),
            pltpu.VMEM((2, BLK, 2 * D), F32),
            pltpu.VMEM((2, BLK, 2 * D), BF16),
            pltpu.VMEM((2, BLK, D), BF16),
            pltpu.VMEM((2, BLK, D), BF16),
            pltpu.SMEM((1, BLK), jnp.int32),
            pltpu.SemaphoreType.DMA((7,)),
            pltpu.SemaphoreType.DMA((6,)),
        ],
        name="stored_order",
    )(order, *mid)


def solution(mesh):
    rows = P(("outer", "inner"), None)
    return jax.shard_map(
        on_device,
        mesh=mesh,
        in_specs=(rows, rows, rows, rows, P(), P()),
        out_specs=(rows, rows, rows),
        check_vma=False,
    )
```

```python
import functools
import math

import jax
import jax.numpy as jnp
from jax import lax
from jax.experimental import pallas as pl
from jax.experimental.pallas import tpu as pltpu
from jax.sharding import PartitionSpec as P

BLK = 128
PAIR = 2 * BLK
D = 128
HEADS = 8
WIDE = HEADS * D
COLS = 2 * HEADS * BLK
NEGATIVE = -1e30
FACTOR = 1.0 / math.sqrt(D)
TO_EXP2 = FACTOR * math.log2(math.e)
MESH = pl.DeviceIdType.MESH
F32 = jnp.float32
BF16 = jnp.bfloat16
SCORE_UNROLL = 4
GRAD_UNROLL = 4
QUERY_UNROLL = 4
PIECES = 2
PIECE = BLK // PIECES


def dot_last(a, b):
    return lax.dot_general(a, b, (((1,), (1,)), ((), ())), preferred_element_type=F32)


def dot_mid(a, b):
    return lax.dot_general(a, b, (((1,), (0,)), ((), ())), preferred_element_type=F32)


def rows_of(j, half):
    if j == 0 and half == 1:
        return BLK, BLK
    if j == 3 and half == 0:
        return 0, BLK
    return 0, PAIR


def position(count, inner):
    device = lax.axis_index("outer") * inner + lax.axis_index("inner")
    core = lax.rem(device, 2)
    worker = lax.div(device, 2) + core * (count - 1 - 2 * lax.div(device, 2))
    return device, core, worker


def keeps_first(order_in, device, core, count):
    low_first = (order_in[2 * device] < count).astype(jnp.int32)
    return low_first + core


def choose(flag, first, second):
    return jnp.where(flag, first, second), jnp.where(flag, second, first)


def main_kernel(
    count,
    inner,
    order_ref,
    docs_ref,
    q_ref,
    k_ref,
    v_ref,
    do_ref,
    dq_mine,
    dq_other,
    own_grad,
    sib_grad,
    g_mine,
    g_other,
    q_in,
    do_in,
    k_in,
    v_in,
    docs_in,
    q_all,
    do_all,
    q_other,
    do_other,
    kv,
    kv_other,
    bias,
    weights,
    grad_prob,
    st_max,
    st_sum,
    st_dot,
    st_scale,
    st_row,
    probs,
    grads,
    key_t,
    g_part,
    g_send,
    g_recv,
    own_keep,
    sib_send,
    dq_send,
    order_in,
    nothing,
    in_sem,
    kv_send_sem,
    kv_recv_sem,
    sib_send_sem,
    sib_recv_sem,
    g_send_sem,
    g_recv_sem,
    out_sem,
):
    device, core, worker = position(count, inner)
    mirror = count - 1 - worker

    def place(u):
        u = lax.rem(u + count, count)
        upper = lax.div(u, count // 2)
        return 2 * u + upper * (2 * count - 1 - 4 * u)

    def coords(dev):
        return (lax.div(dev, inner), lax.rem(dev, inner))

    after = place(worker + 1)
    before = place(worker - 1)
    across = place(mirror + 1)
    sibling = place(mirror)
    has_after = worker < count - 1
    reaches_across = (worker > 0) & (worker != count // 2)
    keeps_across = worker == count // 2

    first_row = jnp.maximum(2 * worker - 6, 0)
    loads = [
        pltpu.make_async_copy(k_ref, k_in, in_sem.at[0]),
        pltpu.make_async_copy(v_ref, v_in, in_sem.at[1]),
        pltpu.make_async_copy(q_ref, q_in, in_sem.at[2]),
        pltpu.make_async_copy(do_ref, do_in, in_sem.at[3]),
        pltpu.make_async_copy(docs_ref.at[pl.ds(first_row, 8)], docs_in, in_sem.at[4]),
        pltpu.make_async_copy(order_ref, order_in, in_sem.at[5]),
    ]
    for load in (loads[0], loads[1], loads[5], loads[2], loads[3], loads[4]):
        load.start()

    barrier = pltpu.get_barrier_semaphore()
    pl.semaphore_signal(barrier, inc=1, device_id=coords(sibling), device_id_type=MESH)

    @pl.when(worker > 0)
    def _():
        pl.semaphore_signal(barrier, inc=1, device_id=coords(before), device_id_type=MESH)

    @pl.when(reaches_across)
    def _():
        pl.semaphore_signal(barrier, inc=1, device_id=coords(across), device_id_type=MESH)

    loads[5].wait()
    flag = jnp.full((1, 1), keeps_first(order_in, device, core, count)) == 1
    loads[0].wait()
    loads[1].wait()
    for lanes, ref in ((slice(0, D), k_in), (slice(D, 2 * D), v_in)):
        mine, other = choose(flag, ref[:BLK], ref[BLK:])
        kv[3 * PAIR : 3 * PAIR + BLK, lanes] = mine
        kv_other[:, lanes] = other

    pl.semaphore_wait(barrier, 1 + has_after.astype(jnp.int32) + reaches_across.astype(jnp.int32))

    def remote(src, dst, send_sem, recv_sem, dev):
        return pltpu.make_async_remote_copy(
            src_ref=src,
            dst_ref=dst,
            send_sem=send_sem,
            recv_sem=recv_sem,
            device_id=coords(dev),
            device_id_type=MESH,
        )

    def piece_rows(k, half, piece):
        return kv.at[pl.ds((3 - k) * PAIR + half * BLK + piece * PIECE, PIECE)]

    def kv_copy(k, half, piece):
        if half and k == 1:
            src, dev = kv_other.at[pl.ds(piece * PIECE, PIECE)], across
        else:
            src, dev = piece_rows(k - 1, half, piece), after
        sems = kv_send_sem.at[k - 1, half, piece], kv_recv_sem.at[k - 1, half, piece]
        return remote(src, piece_rows(k, half, piece), *sems, dev)

    def to_sibling(src, dst, index):
        return remote(src, dst, sib_send_sem.at[index], sib_recv_sem.at[index], sibling)

    @pl.when(has_after)
    def _():
        for piece in range(PIECES):
            kv_copy(1, 0, piece).start()

    @pl.when(reaches_across)
    def _():
        for piece in range(PIECES):
            kv_copy(1, 1, piece).start()

    @pl.when(keeps_across)
    def _():
        for piece in range(PIECES):
            pltpu.make_async_copy(
                kv_other.at[pl.ds(piece * PIECE, PIECE)],
                piece_rows(1, 1, piece),
                kv_recv_sem.at[0, 1, piece],
            ).start()

    nothing[...] = jnp.zeros_like(nothing)
    for k in (1, 2, 3):

        @pl.when(worker < k)
        def _():
            for half in (0, 1):
                for piece in range(PIECES):
                    pltpu.make_async_copy(
                        nothing, piece_rows(k, half, piece), kv_recv_sem.at[k - 1, half, piece]
                    ).start()

    pieces = [pl.ds(piece * PIECE, PIECE) for piece in range(PIECES)]

    @pl.when(worker == count - 1)
    def _():
        for piece, rows in enumerate(pieces):
            pltpu.make_async_copy(nothing, g_mine.at[rows], g_recv_sem.at[0, 0, piece]).start()

    for k in (2, 3):

        @pl.when((worker == count - 1) | (worker < k - 1))
        def _():
            for half in (0, 1):
                for piece, rows in enumerate(pieces):
                    pltpu.make_async_copy(
                        nothing, g_recv.at[k - 2, half, rows], g_recv_sem.at[k - 1, half, piece]
                    ).start()

    @pl.when(worker == 0)
    def _():
        for piece, rows in enumerate(pieces):
            pltpu.make_async_copy(nothing, g_other.at[rows], g_recv_sem.at[0, 1, piece]).start()

    kv_move = to_sibling(kv_other, kv.at[pl.ds(3 * PAIR + BLK, BLK)], 4)
    kv_move.start()

    loads[2].wait()
    loads[3].wait()
    for h in range(HEADS):
        lanes = slice(h * D, (h + 1) * D)
        rows = slice(h * BLK, (h + 1) * BLK)
        q_all[rows], q_other[rows] = choose(flag, q_in[:BLK, lanes], q_in[BLK:, lanes])
        do_all[rows], do_other[rows] = choose(flag, do_in[:BLK, lanes], do_in[BLK:, lanes])
    q_move = to_sibling(q_other, q_all.at[pl.ds(COLS // 2, COLS // 2)], 0)
    do_move = to_sibling(do_other, do_all.at[pl.ds(COLS // 2, COLS // 2)], 1)
    q_move.start()
    do_move.start()

    loads[4].wait()
    key_iota = lax.broadcasted_iota(jnp.int32, (BLK, BLK), 0)
    query_iota = lax.broadcasted_iota(jnp.int32, (BLK, BLK), 1)

    def doc_row(window_block):
        block = 2 * worker - 6 + window_block
        return docs_in[jnp.maximum(block, 0) - first_row]

    def make_masks(blocks):
        query_docs = [jnp.broadcast_to(doc_row(6 + half), (BLK, BLK)) for half in (0, 1)]
        for block in blocks:
            key_docs = jnp.broadcast_to(doc_row(block).astype(F32), (BLK, BLK)).T.astype(jnp.int32)
            key_docs = jnp.where(2 * worker - 6 + block >= 0, key_docs, -1)
            for half in (0, 1):
                if block < half or block > 6 + half:
                    continue
                allowed = key_docs == query_docs[half]
                if block == 6 + half:
                    allowed = allowed & (key_iota <= query_iota)
                if block == half:
                    allowed = allowed & (key_iota > query_iota)
                bias[half, block * BLK : (block + 1) * BLK] = jnp.where(allowed, 0.0, NEGATIVE)

    def scores(j, half):
        first, rows = rows_of(j, half)
        begin = j * PAIR + first

        def step(i, carry):
            t = half * 4 + i
            lanes = pl.ds(pl.multiple_of(t * PAIR, PAIR), PAIR)
            mask = bias[half, begin : begin + rows]
            s = dot_last(kv[begin : begin + rows, :D], q_all[lanes])
            s = s + jnp.concatenate([mask, mask], 1)
            g = dot_last(kv[begin : begin + rows, D:], do_all[lanes])
            top = jnp.max(s, axis=0, keepdims=True)
            e = jnp.exp2((s - top) * TO_EXP2)
            weights[j, t, first : first + rows] = e
            grad_prob[j, t, first : first + rows] = g
            st_max[j, t] = jnp.broadcast_to(top, (8, PAIR))
            st_sum[j, t] = jnp.sum(e.reshape(rows // 8, 8, PAIR), axis=0)
            st_dot[j, t] = jnp.sum((e * g).reshape(rows // 8, 8, PAIR), axis=0)
            return carry

        lax.fori_loop(0, 4, step, 0, unroll=SCORE_UNROLL)

    def transpose_keys(j):
        begin = j * PAIR
        key_t[:, begin : begin + PAIR] = kv[begin : begin + PAIR, :D].astype(F32).T.astype(BF16)

    def pass_on(k):
        for half in (0, 1):
            for piece in range(PIECES):
                kv_copy(k, half, piece).wait_recv()

                @pl.when(has_after & (worker >= k))
                def _():
                    kv_copy(k + 1, half, piece).start()

    make_masks((6, 7))
    scores(3, 0)
    kv_move.wait_recv()
    make_masks((4, 5))
    pass_on(1)
    transpose_keys(3)
    q_move.wait_recv()
    do_move.wait_recv()
    scores(3, 1)
    scores(2, 0)
    pass_on(2)
    make_masks((0, 1, 2, 3))
    scores(2, 1)
    transpose_keys(2)
    scores(1, 0)
    scores(1, 1)
    transpose_keys(1)
    for half in (0, 1):
        for piece in range(PIECES):
            kv_copy(3, half, piece).wait_recv()
    scores(0, 0)
    scores(0, 1)

    def finish_stats(t, carry):
        tops = [st_max[j, t] for j in range(4)]
        top = jnp.maximum(jnp.maximum(tops[0], tops[1]), jnp.maximum(tops[2], tops[3]))
        scales = [jnp.exp2((tops[j] - top) * TO_EXP2) for j in range(4)]
        total = sum(st_sum[j, t] * scales[j] for j in range(4))
        dotted = sum(st_dot[j, t] * scales[j] for j in range(4))
        inverse = 1.0 / jnp.sum(total, axis=0, keepdims=True)
        row = jnp.sum(dotted, axis=0, keepdims=True) * inverse
        for j in range(4):
            st_scale[j, t] = scales[j] * inverse
        st_row[t] = jnp.broadcast_to(row, (8, PAIR))
        return carry

    lax.fori_loop(0, 8, finish_stats, 0, unroll=4)

    def grads_of(j):
        for half in (0, 1):
            first, rows = rows_of(j, half)

            def step(i, carry):
                t = half * 4 + i
                lanes = pl.ds(pl.multiple_of(t * PAIR, PAIR), PAIR)
                tall = (rows // 8, 8, PAIR)
                p = weights[j, t, first : first + rows].reshape(tall) * st_scale[j, t][None]
                g = grad_prob[j, t, first : first + rows].reshape(tall) - st_row[t][None]
                ds = (p * g).reshape(rows, PAIR)
                probs[first : first + rows, lanes] = p.reshape(rows, PAIR).astype(BF16)
                grads[j * PAIR + first : j * PAIR + first + rows, lanes] = ds.astype(BF16)
                return carry

            lax.fori_loop(0, 4, step, 0, unroll=GRAD_UNROLL)

    def key_value_grads(j, half):
        lane, lanes = 0, COLS
        if j == 0 and half == 0:
            lanes = COLS // 2
        if j == 3 and half == 1:
            lane, lanes = COLS // 2, COLS // 2
        first = half * BLK
        begin = j * PAIR + first
        gk = dot_mid(grads[begin : begin + BLK, lane : lane + lanes], q_all[lane : lane + lanes])
        gv = dot_mid(probs[first : first + BLK, lane : lane + lanes], do_all[lane : lane + lanes])
        return gk, gv

    def g_copy(k, half, piece):
        rows = pl.ds(piece * PIECE, PIECE)
        if k > 1:
            dst, dev = g_recv.at[k - 2, half, rows], before
        elif half:
            dst, dev = g_other.at[rows], across
        else:
            dst, dev = g_mine.at[rows], before
        sems = g_send_sem.at[k - 1, half, piece], g_recv_sem.at[k - 1, half, piece]
        return remote(g_send.at[k - 1, half, rows], dst, *sems, dev)

    grads_of(0)
    for half in (0, 1):
        gk, gv = key_value_grads(0, half)
        g_send[2, half, :, :D] = gk.astype(BF16)
        g_send[2, half, :, D:] = gv.astype(BF16)

        @pl.when(worker >= 3)
        def _():
            for piece in range(PIECES):
                g_copy(3, half, piece).start()

    def part_of(k):
        grads_of(3 - k)
        for half in (0, 1):
            gk, gv = key_value_grads(3 - k, half)
            g_part[k - 1, half, :, :D] = gk
            g_part[k - 1, half, :, D:] = gv

    def add_and_send(k):
        for half in (0, 1):
            for piece in range(PIECES):
                rows = pl.ds(piece * PIECE, PIECE)
                g_copy(k + 1, half, piece).wait_recv()
                total = g_part[k - 1, half, rows] + g_recv[k - 1, half, rows].astype(F32)
                g_send[k - 1, half, rows] = total.astype(BF16)
                if k == 1 and half == 1:

                    @pl.when(reaches_across)
                    def _():
                        g_copy(1, 1, piece).start()

                    @pl.when(keeps_across)
                    def _():
                        pltpu.make_async_copy(
                            g_send.at[0, 1, rows], g_other.at[rows], g_recv_sem.at[0, 1, piece]
                        ).start()
                else:

                    @pl.when(worker >= k)
                    def _():
                        g_copy(k, half, piece).start()

    def query_grads(half, emit):
        begin = half * BLK

        def step(i, carry):
            lanes = pl.ds(pl.multiple_of((half * 4 + i) * PAIR, PAIR), PAIR)
            g = dot_mid(key_t[:, begin : begin + 7 * BLK], grads[begin : begin + 7 * BLK, lanes])
            g = g * FACTOR
            for side in (0, 1):
                head = pl.ds(pl.multiple_of((i * 2 + side) * D, D), D)
                dq_send[half, :, head] = g[:, side * BLK : (side + 1) * BLK].T.astype(BF16)
            return carry

        lax.fori_loop(0, 4, step, 0, unroll=QUERY_UNROLL)

    part_of(2)
    part_of(1)
    add_and_send(2)
    transpose_keys(0)
    grads_of(3)
    gk, gv = key_value_grads(3, 1)
    sib_send[:, :D] = gk
    sib_send[:, D:] = gv
    sib_move = to_sibling(sib_send, sib_grad, 2)
    sib_move.start()
    gk, gv = key_value_grads(3, 0)
    own_keep[:, :D] = gk
    own_keep[:, D:] = gv
    own_out = pltpu.make_async_copy(own_keep, own_grad, out_sem.at[0])
    own_out.start()
    query_grads(1, None)
    dq_move = to_sibling(dq_send.at[1], dq_other, 3)
    dq_move.start()
    add_and_send(1)
    query_grads(0, None)
    dq_out = pltpu.make_async_copy(dq_send.at[0], dq_mine, out_sem.at[1])
    dq_out.start()

    own_out.wait()
    for move in (q_move, do_move, kv_move, sib_move, dq_move):
        move.wait_send()
    for k in (1, 2, 3):
        for half in (0, 1):
            sends = reaches_across if k == 1 and half == 1 else worker >= k

            @pl.when(sends)
            def _():
                for piece in range(PIECES):
                    g_copy(k, half, piece).wait_send()

            if not (k == 1 and half == 1):
                sends = has_after & (worker >= k - 1)

            @pl.when(sends)
            def _():
                for piece in range(PIECES):
                    kv_copy(k, half, piece).wait_send()
    sib_move.wait_recv()
    dq_out.wait()
    dq_move.wait_recv()
    for half in (0, 1):
        for piece in range(PIECES):
            g_copy(1, half, piece).wait_recv()


def last_kernel(
    count,
    inner,
    order_ref,
    dq_mine,
    dq_other,
    own_grad,
    sib_grad,
    g_mine,
    g_other,
    dq_ref,
    dk_ref,
    dv_ref,
    dq_in,
    near_in,
    far_in,
    dk_out,
    dv_out,
    order_in,
    in_sem,
    out_sem,
):
    device, core, _ = position(count, inner)
    order = pltpu.make_async_copy(order_ref, order_in, in_sem.at[6])
    loads = [
        pltpu.make_async_copy(dq_mine, dq_in.at[0], in_sem.at[0]),
        pltpu.make_async_copy(dq_other, dq_in.at[1], in_sem.at[1]),
        pltpu.make_async_copy(own_grad, near_in.at[0], in_sem.at[2]),
        pltpu.make_async_copy(g_mine, far_in.at[0], in_sem.at[3]),
        pltpu.make_async_copy(sib_grad, near_in.at[1], in_sem.at[4]),
        pltpu.make_async_copy(g_other, far_in.at[1], in_sem.at[5]),
    ]
    order.start()
    for load in loads:
        load.start()
    order.wait()
    mine_slot = jnp.where(keeps_first(order_in, device, core, count) == 1, 0, 1)
    stores = []
    for which in (0, 1):
        slot = mine_slot if which == 0 else 1 - mine_slot
        rows = pl.ds(pl.multiple_of(slot * BLK, BLK), BLK)
        loads[which].wait()
        stores.append(pltpu.make_async_copy(dq_in.at[which], dq_ref.at[rows], out_sem.at[3 * which]))
        stores[-1].start()
    for which in (0, 1):
        slot = mine_slot if which == 0 else 1 - mine_slot
        rows = pl.ds(pl.multiple_of(slot * BLK, BLK), BLK)
        loads[2 + 2 * which].wait()
        loads[3 + 2 * which].wait()
        total = near_in[which] + far_in[which].astype(F32)
        dk_out[which] = (total[:, :D] * FACTOR).astype(BF16)
        dv_out[which] = total[:, D:].astype(BF16)
        for step, (src, dst) in enumerate(((dk_out, dk_ref), (dv_out, dv_ref))):
            sem = out_sem.at[3 * which + 1 + step]
            stores.append(pltpu.make_async_copy(src.at[which], dst.at[rows], sem))
            stores[-1].start()
    for store in stores:
        store.wait()


def on_device(queries, key_states, value_states, grad_output, documents, block_order):
    inner = lax.axis_size("inner")
    count = lax.axis_size("outer") * inner
    hbm = pl.BlockSpec(memory_space=pl.ANY)
    docs = documents.reshape(2 * count, 1, BLK)
    mid = pl.pallas_call(
        functools.partial(main_kernel, count, inner),
        out_shape=[
            jax.ShapeDtypeStruct((BLK, WIDE), BF16),
            jax.ShapeDtypeStruct((BLK, WIDE), BF16),
            jax.ShapeDtypeStruct((BLK, 2 * D), F32),
            jax.ShapeDtypeStruct((BLK, 2 * D), F32),
            jax.ShapeDtypeStruct((BLK, 2 * D), BF16),
            jax.ShapeDtypeStruct((BLK, 2 * D), BF16),
        ],
        in_specs=[hbm] * 6,
        out_specs=[hbm] * 6,
        scratch_shapes=[
            pltpu.VMEM((PAIR, WIDE), BF16),
            pltpu.VMEM((PAIR, WIDE), BF16),
            pltpu.VMEM((PAIR, D), BF16),
            pltpu.VMEM((PAIR, D), BF16),
            pltpu.VMEM((8, 1, BLK), jnp.int32),
            pltpu.VMEM((COLS, D), BF16),
            pltpu.VMEM((COLS, D), BF16),
            pltpu.VMEM((COLS // 2, D), BF16),
            pltpu.VMEM((COLS // 2, D), BF16),
            pltpu.VMEM((4 * PAIR, 2 * D), BF16),
            pltpu.VMEM((BLK, 2 * D), BF16),
            pltpu.VMEM((2, 4 * PAIR, BLK), F32),
            pltpu.VMEM((4, 8, PAIR, PAIR), F32),
            pltpu.VMEM((4, 8, PAIR, PAIR), F32),
            pltpu.VMEM((4, 8, 8, PAIR), F32),
            pltpu.VMEM((4, 8, 8, PAIR), F32),
            pltpu.VMEM((4, 8, 8, PAIR), F32),
            pltpu.VMEM((4, 8, 8, PAIR), F32),
            pltpu.VMEM((8, 8, PAIR), F32),
            pltpu.VMEM((PAIR, COLS), BF16),
            pltpu.VMEM((4 * PAIR, COLS), BF16),
            pltpu.VMEM((D, 4 * PAIR), BF16),
            pltpu.VMEM((2, 2, BLK, 2 * D), F32),
            pltpu.VMEM((3, 2, BLK, 2 * D), BF16),
            pltpu.VMEM((2, 2, BLK, 2 * D), BF16),
            pltpu.VMEM((BLK, 2 * D), F32),
            pltpu.VMEM((BLK, 2 * D), F32),
            pltpu.VMEM((2, BLK, WIDE), BF16),
            pltpu.SMEM((2 * count,), jnp.int32),
            pltpu.VMEM((PIECE, 2 * D), BF16),
            pltpu.SemaphoreType.DMA((6,)),
            pltpu.SemaphoreType.DMA((3, 2, PIECES)),
            pltpu.SemaphoreType.DMA((3, 2, PIECES)),
            pltpu.SemaphoreType.DMA((5,)),
            pltpu.SemaphoreType.DMA((5,)),
            pltpu.SemaphoreType.DMA((3, 2, PIECES)),
            pltpu.SemaphoreType.DMA((3, 2, PIECES)),
            pltpu.SemaphoreType.DMA((2,)),
        ],
        compiler_params=pltpu.CompilerParams(
            collective_id=0, has_side_effects=True, vmem_limit_bytes=60 * 1024 * 1024
        ),
        name="attention_backward",
    )(block_order, docs, queries, key_states, value_states, grad_output)
    return pl.pallas_call(
        functools.partial(last_kernel, count, inner),
        out_shape=[
            jax.ShapeDtypeStruct((PAIR, WIDE), BF16),
            jax.ShapeDtypeStruct((PAIR, D), BF16),
            jax.ShapeDtypeStruct((PAIR, D), BF16),
        ],
        in_specs=[hbm] * 7,
        out_specs=[hbm] * 3,
        scratch_shapes=[
            pltpu.VMEM((2, BLK, WIDE), BF16),
            pltpu.VMEM((2, BLK, 2 * D), F32),
            pltpu.VMEM((2, BLK, 2 * D), BF16),
            pltpu.VMEM((2, BLK, D), BF16),
            pltpu.VMEM((2, BLK, D), BF16),
            pltpu.SMEM((2 * count,), jnp.int32),
            pltpu.SemaphoreType.DMA((7,)),
            pltpu.SemaphoreType.DMA((6,)),
        ],
        name="stored_order",
    )(block_order, *mid)


def solution(mesh):
    rows = P(("outer", "inner"), None)
    return jax.shard_map(
        on_device,
        mesh=mesh,
        in_specs=(rows, rows, rows, rows, P(), P()),
        out_specs=(rows, rows, rows),
        check_vma=False,
    )
```

```python
import functools
import math

import jax
import jax.numpy as jnp
from jax import lax
from jax.experimental import pallas as pl
from jax.experimental.pallas import tpu as pltpu
from jax.sharding import PartitionSpec as P

BLK = 128
PAIR = 2 * BLK
D = 128
HEADS = 8
WIDE = HEADS * D
COLS = 2 * HEADS * BLK
NEGATIVE = -1e30
FACTOR = 1.0 / math.sqrt(D)
TO_EXP2 = FACTOR * math.log2(math.e)
MESH = pl.DeviceIdType.MESH
F32 = jnp.float32
BF16 = jnp.bfloat16
SCORE_UNROLL = 4
GRAD_UNROLL = 4
QUERY_UNROLL = 4
PIECES = 2
PIECE = BLK // PIECES


def dot_last(a, b):
    return lax.dot_general(a, b, (((1,), (1,)), ((), ())), preferred_element_type=F32)


def dot_mid(a, b):
    return lax.dot_general(a, b, (((1,), (0,)), ((), ())), preferred_element_type=F32)


def rows_of(j, half):
    if j == 0 and half == 1:
        return BLK, BLK
    if j == 3 and half == 0:
        return 0, BLK
    return 0, PAIR


def position(count, inner):
    device = lax.axis_index("outer") * inner + lax.axis_index("inner")
    core = lax.rem(device, 2)
    worker = lax.div(device, 2) + core * (count - 1 - 2 * lax.div(device, 2))
    return device, core, worker


def keeps_first(order_in, device, core, count):
    low_first = (order_in[2 * device] < count).astype(jnp.int32)
    return low_first + core


def choose(flag, first, second):
    return jnp.where(flag, first, second), jnp.where(flag, second, first)


def main_kernel(
    count,
    inner,
    order_ref,
    docs_ref,
    q_ref,
    k_ref,
    v_ref,
    do_ref,
    dq_mine,
    dq_other,
    own_grad,
    sib_grad,
    g_mine,
    g_other,
    q_in,
    do_in,
    k_in,
    v_in,
    docs_in,
    q_all,
    do_all,
    q_other,
    do_other,
    kv,
    kv_other,
    bias,
    weights,
    grad_prob,
    st_max,
    st_sum,
    st_dot,
    st_scale,
    st_row,
    probs,
    grads,
    key_t,
    g_part,
    g_send,
    g_recv,
    own_keep,
    sib_send,
    dq_send,
    order_in,
    nothing,
    in_sem,
    kv_send_sem,
    kv_recv_sem,
    sib_send_sem,
    sib_recv_sem,
    g_send_sem,
    g_recv_sem,
    out_sem,
):
    device, core, worker = position(count, inner)
    mirror = count - 1 - worker

    def place(u):
        u = lax.rem(u + count, count)
        upper = lax.div(u, count // 2)
        return 2 * u + upper * (2 * count - 1 - 4 * u)

    def coords(dev):
        return (lax.div(dev, inner), lax.rem(dev, inner))

    after = place(worker + 1)
    before = place(worker - 1)
    across = place(mirror + 1)
    sibling = place(mirror)
    has_after = worker < count - 1
    reaches_across = (worker > 0) & (worker != count // 2)
    keeps_across = worker == count // 2

    first_row = jnp.maximum(2 * worker - 6, 0)
    loads = [
        pltpu.make_async_copy(k_ref, k_in, in_sem.at[0]),
        pltpu.make_async_copy(v_ref, v_in, in_sem.at[1]),
        pltpu.make_async_copy(q_ref, q_in, in_sem.at[2]),
        pltpu.make_async_copy(do_ref, do_in, in_sem.at[3]),
        pltpu.make_async_copy(docs_ref.at[pl.ds(first_row, 8)], docs_in, in_sem.at[4]),
        pltpu.make_async_copy(order_ref, order_in, in_sem.at[5]),
    ]
    for load in (loads[0], loads[1], loads[5], loads[2], loads[3], loads[4]):
        load.start()

    barrier = pltpu.get_barrier_semaphore()
    pl.semaphore_signal(barrier, inc=1, device_id=coords(sibling), device_id_type=MESH)

    @pl.when(worker > 0)
    def _():
        pl.semaphore_signal(barrier, inc=1, device_id=coords(before), device_id_type=MESH)

    @pl.when(reaches_across)
    def _():
        pl.semaphore_signal(barrier, inc=1, device_id=coords(across), device_id_type=MESH)

    loads[5].wait()
    flag = jnp.full((1, 1), keeps_first(order_in, device, core, count)) == 1
    loads[0].wait()
    loads[1].wait()
    for lanes, ref in ((slice(0, D), k_in), (slice(D, 2 * D), v_in)):
        mine, other = choose(flag, ref[:BLK], ref[BLK:])
        kv[3 * PAIR : 3 * PAIR + BLK, lanes] = mine
        kv_other[:, lanes] = other

    pl.semaphore_wait(barrier, 1 + has_after.astype(jnp.int32) + reaches_across.astype(jnp.int32))

    def remote(src, dst, send_sem, recv_sem, dev):
        return pltpu.make_async_remote_copy(
            src_ref=src,
            dst_ref=dst,
            send_sem=send_sem,
            recv_sem=recv_sem,
            device_id=coords(dev),
            device_id_type=MESH,
        )

    def piece_rows(k, half, piece):
        return kv.at[pl.ds((3 - k) * PAIR + half * BLK + piece * PIECE, PIECE)]

    def kv_copy(k, half, piece):
        if half and k == 1:
            src, dev = kv_other.at[pl.ds(piece * PIECE, PIECE)], across
        else:
            src, dev = piece_rows(k - 1, half, piece), after
        sems = kv_send_sem.at[k - 1, half, piece], kv_recv_sem.at[k - 1, half, piece]
        return remote(src, piece_rows(k, half, piece), *sems, dev)

    def to_sibling(src, dst, index):
        return remote(src, dst, sib_send_sem.at[index], sib_recv_sem.at[index], sibling)

    @pl.when(has_after)
    def _():
        for piece in range(PIECES):
            kv_copy(1, 0, piece).start()

    @pl.when(reaches_across)
    def _():
        for piece in range(PIECES):
            kv_copy(1, 1, piece).start()

    @pl.when(keeps_across)
    def _():
        for piece in range(PIECES):
            pltpu.make_async_copy(
                kv_other.at[pl.ds(piece * PIECE, PIECE)],
                piece_rows(1, 1, piece),
                kv_recv_sem.at[0, 1, piece],
            ).start()

    nothing[...] = jnp.zeros_like(nothing)
    for k in (1, 2, 3):

        @pl.when(worker < k)
        def _():
            for half in (0, 1):
                for piece in range(PIECES):
                    pltpu.make_async_copy(
                        nothing, piece_rows(k, half, piece), kv_recv_sem.at[k - 1, half, piece]
                    ).start()

    pieces = [pl.ds(piece * PIECE, PIECE) for piece in range(PIECES)]

    @pl.when(worker == count - 1)
    def _():
        for piece, rows in enumerate(pieces):
            pltpu.make_async_copy(nothing, g_mine.at[rows], g_recv_sem.at[0, 0, piece]).start()

    for k in (2, 3):

        @pl.when((worker == count - 1) | (worker < k - 1))
        def _():
            for half in (0, 1):
                for piece, rows in enumerate(pieces):
                    pltpu.make_async_copy(
                        nothing, g_recv.at[k - 2, half, rows], g_recv_sem.at[k - 1, half, piece]
                    ).start()

    @pl.when(worker == 0)
    def _():
        for piece, rows in enumerate(pieces):
            pltpu.make_async_copy(nothing, g_other.at[rows], g_recv_sem.at[0, 1, piece]).start()

    kv_move = to_sibling(kv_other, kv.at[pl.ds(3 * PAIR + BLK, BLK)], 4)
    kv_move.start()

    loads[2].wait()
    loads[3].wait()
    for h in range(HEADS):
        lanes = slice(h * D, (h + 1) * D)
        rows = slice(h * BLK, (h + 1) * BLK)
        q_all[rows], q_other[rows] = choose(flag, q_in[:BLK, lanes], q_in[BLK:, lanes])
        do_all[rows], do_other[rows] = choose(flag, do_in[:BLK, lanes], do_in[BLK:, lanes])
    q_move = to_sibling(q_other, q_all.at[pl.ds(COLS // 2, COLS // 2)], 0)
    do_move = to_sibling(do_other, do_all.at[pl.ds(COLS // 2, COLS // 2)], 1)
    q_move.start()
    do_move.start()

    loads[4].wait()
    key_iota = lax.broadcasted_iota(jnp.int32, (BLK, BLK), 0)
    query_iota = lax.broadcasted_iota(jnp.int32, (BLK, BLK), 1)

    def doc_row(window_block):
        block = 2 * worker - 6 + window_block
        return docs_in[jnp.maximum(block, 0) - first_row]

    def make_masks(blocks):
        query_docs = [jnp.broadcast_to(doc_row(6 + half), (BLK, BLK)) for half in (0, 1)]
        for block in blocks:
            key_docs = jnp.broadcast_to(doc_row(block).astype(F32), (BLK, BLK)).T.astype(jnp.int32)
            key_docs = jnp.where(2 * worker - 6 + block >= 0, key_docs, -1)
            for half in (0, 1):
                if block < half or block > 6 + half:
                    continue
                allowed = key_docs == query_docs[half]
                if block == 6 + half:
                    allowed = allowed & (key_iota <= query_iota)
                if block == half:
                    allowed = allowed & (key_iota > query_iota)
                bias[half, block * BLK : (block + 1) * BLK] = jnp.where(allowed, 0.0, NEGATIVE)

    def scores(j, half):
        first, rows = rows_of(j, half)
        begin = j * PAIR + first

        def step(i, carry):
            t = half * 4 + i
            lanes = pl.ds(pl.multiple_of(t * PAIR, PAIR), PAIR)
            mask = bias[half, begin : begin + rows]
            s = dot_last(kv[begin : begin + rows, :D], q_all[lanes])
            s = s + jnp.concatenate([mask, mask], 1)
            g = dot_last(kv[begin : begin + rows, D:], do_all[lanes])
            top = jnp.max(s, axis=0, keepdims=True)
            e = jnp.exp2((s - top) * TO_EXP2)
            weights[j, t, first : first + rows] = e
            grad_prob[j, t, first : first + rows] = g
            st_max[j, t] = jnp.broadcast_to(top, (8, PAIR))
            st_sum[j, t] = jnp.sum(e.reshape(rows // 8, 8, PAIR), axis=0)
            st_dot[j, t] = jnp.sum((e * g).reshape(rows // 8, 8, PAIR), axis=0)
            return carry

        lax.fori_loop(0, 4, step, 0, unroll=SCORE_UNROLL)

    def transpose_keys(j):
        begin = j * PAIR
        key_t[:, begin : begin + PAIR] = kv[begin : begin + PAIR, :D].astype(F32).T.astype(BF16)

    def pass_on(k):
        for half in (0, 1):
            for piece in range(PIECES):
                kv_copy(k, half, piece).wait_recv()

                @pl.when(has_after & (worker >= k))
                def _():
                    kv_copy(k + 1, half, piece).start()

    make_masks((6, 7))
    scores(3, 0)
    kv_move.wait_recv()
    make_masks((4, 5))
    pass_on(1)
    transpose_keys(3)
    q_move.wait_recv()
    do_move.wait_recv()
    scores(3, 1)
    scores(2, 0)
    pass_on(2)
    make_masks((0, 1, 2, 3))
    scores(2, 1)
    transpose_keys(2)
    scores(1, 0)
    scores(1, 1)
    transpose_keys(1)
    for half in (0, 1):
        for piece in range(PIECES):
            kv_copy(3, half, piece).wait_recv()
    scores(0, 0)
    scores(0, 1)

    def finish_stats(t, carry):
        tops = [st_max[j, t] for j in range(4)]
        top = jnp.maximum(jnp.maximum(tops[0], tops[1]), jnp.maximum(tops[2], tops[3]))
        scales = [jnp.exp2((tops[j] - top) * TO_EXP2) for j in range(4)]
        total = sum(st_sum[j, t] * scales[j] for j in range(4))
        dotted = sum(st_dot[j, t] * scales[j] for j in range(4))
        inverse = 1.0 / jnp.sum(total, axis=0, keepdims=True)
        row = jnp.sum(dotted, axis=0, keepdims=True) * inverse
        for j in range(4):
            st_scale[j, t] = scales[j] * inverse
        st_row[t] = jnp.broadcast_to(row, (8, PAIR))
        return carry

    lax.fori_loop(0, 8, finish_stats, 0, unroll=4)

    def grads_of(j, halves=(0, 1)):
        for half in halves:
            first, rows = rows_of(j, half)

            def step(i, carry):
                t = half * 4 + i
                lanes = pl.ds(pl.multiple_of(t * PAIR, PAIR), PAIR)
                tall = (rows // 8, 8, PAIR)
                p = weights[j, t, first : first + rows].reshape(tall) * st_scale[j, t][None]
                g = grad_prob[j, t, first : first + rows].reshape(tall) - st_row[t][None]
                ds = (p * g).reshape(rows, PAIR)
                probs[first : first + rows, lanes] = p.reshape(rows, PAIR).astype(BF16)
                grads[j * PAIR + first : j * PAIR + first + rows, lanes] = ds.astype(BF16)
                return carry

            lax.fori_loop(0, 4, step, 0, unroll=GRAD_UNROLL)

    def key_value_grads(j, half):
        lane, lanes = 0, COLS
        if j == 0 and half == 0:
            lanes = COLS // 2
        if j == 3 and half == 1:
            lane, lanes = COLS // 2, COLS // 2
        first = half * BLK
        begin = j * PAIR + first
        gk = dot_mid(grads[begin : begin + BLK, lane : lane + lanes], q_all[lane : lane + lanes])
        gv = dot_mid(probs[first : first + BLK, lane : lane + lanes], do_all[lane : lane + lanes])
        return gk, gv

    def g_copy(k, half, piece):
        rows = pl.ds(piece * PIECE, PIECE)
        if k > 1:
            dst, dev = g_recv.at[k - 2, half, rows], before
        elif half:
            dst, dev = g_other.at[rows], across
        else:
            dst, dev = g_mine.at[rows], before
        sems = g_send_sem.at[k - 1, half, piece], g_recv_sem.at[k - 1, half, piece]
        return remote(g_send.at[k - 1, half, rows], dst, *sems, dev)

    for half in (0, 1):
        grads_of(0, (half,))
        gk, gv = key_value_grads(0, half)
        g_send[2, half, :, :D] = gk.astype(BF16)
        g_send[2, half, :, D:] = gv.astype(BF16)

        @pl.when(worker >= 3)
        def _():
            for piece in range(PIECES):
                g_copy(3, half, piece).start()

    def part_of(k):
        grads_of(3 - k)
        for half in (0, 1):
            gk, gv = key_value_grads(3 - k, half)
            g_part[k - 1, half, :, :D] = gk
            g_part[k - 1, half, :, D:] = gv

    def add_and_send(k):
        for half in (0, 1):
            for piece in range(PIECES):
                rows = pl.ds(piece * PIECE, PIECE)
                g_copy(k + 1, half, piece).wait_recv()
                total = g_part[k - 1, half, rows] + g_recv[k - 1, half, rows].astype(F32)
                g_send[k - 1, half, rows] = total.astype(BF16)
                if k == 1 and half == 1:

                    @pl.when(reaches_across)
                    def _():
                        g_copy(1, 1, piece).start()

                    @pl.when(keeps_across)
                    def _():
                        pltpu.make_async_copy(
                            g_send.at[0, 1, rows], g_other.at[rows], g_recv_sem.at[0, 1, piece]
                        ).start()
                else:

                    @pl.when(worker >= k)
                    def _():
                        g_copy(k, half, piece).start()

    def query_grads(half, emit):
        begin = half * BLK

        def step(i, carry):
            lanes = pl.ds(pl.multiple_of((half * 4 + i) * PAIR, PAIR), PAIR)
            g = dot_mid(key_t[:, begin : begin + 7 * BLK], grads[begin : begin + 7 * BLK, lanes])
            g = g * FACTOR
            for side in (0, 1):
                head = pl.ds(pl.multiple_of((i * 2 + side) * D, D), D)
                dq_send[half, :, head] = g[:, side * BLK : (side + 1) * BLK].T.astype(BF16)
            return carry

        lax.fori_loop(0, 4, step, 0, unroll=QUERY_UNROLL)

    part_of(2)
    part_of(1)
    add_and_send(2)
    transpose_keys(0)
    grads_of(3)
    gk, gv = key_value_grads(3, 1)
    sib_send[:, :D] = gk
    sib_send[:, D:] = gv
    sib_move = to_sibling(sib_send, sib_grad, 2)
    sib_move.start()
    gk, gv = key_value_grads(3, 0)
    own_keep[:, :D] = gk
    own_keep[:, D:] = gv
    own_out = pltpu.make_async_copy(own_keep, own_grad, out_sem.at[0])
    own_out.start()
    query_grads(1, None)
    dq_move = to_sibling(dq_send.at[1], dq_other, 3)
    dq_move.start()
    add_and_send(1)
    query_grads(0, None)
    dq_out = pltpu.make_async_copy(dq_send.at[0], dq_mine, out_sem.at[1])
    dq_out.start()

    own_out.wait()
    for move in (q_move, do_move, kv_move, sib_move, dq_move):
        move.wait_send()
    for k in (1, 2, 3):
        for half in (0, 1):
            sends = reaches_across if k == 1 and half == 1 else worker >= k

            @pl.when(sends)
            def _():
                for piece in range(PIECES):
                    g_copy(k, half, piece).wait_send()

            if not (k == 1 and half == 1):
                sends = has_after & (worker >= k - 1)

            @pl.when(sends)
            def _():
                for piece in range(PIECES):
                    kv_copy(k, half, piece).wait_send()
    sib_move.wait_recv()
    dq_out.wait()
    dq_move.wait_recv()
    for half in (0, 1):
        for piece in range(PIECES):
            g_copy(1, half, piece).wait_recv()


def last_kernel(
    count,
    inner,
    order_ref,
    dq_mine,
    dq_other,
    own_grad,
    sib_grad,
    g_mine,
    g_other,
    dq_ref,
    dk_ref,
    dv_ref,
    dq_in,
    near_in,
    far_in,
    dk_out,
    dv_out,
    order_in,
    in_sem,
    out_sem,
):
    device, core, _ = position(count, inner)
    order = pltpu.make_async_copy(order_ref, order_in, in_sem.at[6])
    loads = [
        pltpu.make_async_copy(dq_mine, dq_in.at[0], in_sem.at[0]),
        pltpu.make_async_copy(dq_other, dq_in.at[1], in_sem.at[1]),
        pltpu.make_async_copy(own_grad, near_in.at[0], in_sem.at[2]),
        pltpu.make_async_copy(g_mine, far_in.at[0], in_sem.at[3]),
        pltpu.make_async_copy(sib_grad, near_in.at[1], in_sem.at[4]),
        pltpu.make_async_copy(g_other, far_in.at[1], in_sem.at[5]),
    ]
    order.start()
    for load in loads:
        load.start()
    order.wait()
    mine_slot = jnp.where(keeps_first(order_in, device, core, count) == 1, 0, 1)
    stores = []
    for which in (0, 1):
        slot = mine_slot if which == 0 else 1 - mine_slot
        rows = pl.ds(pl.multiple_of(slot * BLK, BLK), BLK)
        loads[which].wait()
        stores.append(pltpu.make_async_copy(dq_in.at[which], dq_ref.at[rows], out_sem.at[3 * which]))
        stores[-1].start()
    for which in (0, 1):
        slot = mine_slot if which == 0 else 1 - mine_slot
        rows = pl.ds(pl.multiple_of(slot * BLK, BLK), BLK)
        loads[2 + 2 * which].wait()
        loads[3 + 2 * which].wait()
        total = near_in[which] + far_in[which].astype(F32)
        dk_out[which] = (total[:, :D] * FACTOR).astype(BF16)
        dv_out[which] = total[:, D:].astype(BF16)
        for step, (src, dst) in enumerate(((dk_out, dk_ref), (dv_out, dv_ref))):
            sem = out_sem.at[3 * which + 1 + step]
            stores.append(pltpu.make_async_copy(src.at[which], dst.at[rows], sem))
            stores[-1].start()
    for store in stores:
        store.wait()


def on_device(queries, key_states, value_states, grad_output, documents, block_order):
    inner = lax.axis_size("inner")
    count = lax.axis_size("outer") * inner
    hbm = pl.BlockSpec(memory_space=pl.ANY)
    docs = documents.reshape(2 * count, 1, BLK)
    mid = pl.pallas_call(
        functools.partial(main_kernel, count, inner),
        out_shape=[
            jax.ShapeDtypeStruct((BLK, WIDE), BF16),
            jax.ShapeDtypeStruct((BLK, WIDE), BF16),
            jax.ShapeDtypeStruct((BLK, 2 * D), F32),
            jax.ShapeDtypeStruct((BLK, 2 * D), F32),
            jax.ShapeDtypeStruct((BLK, 2 * D), BF16),
            jax.ShapeDtypeStruct((BLK, 2 * D), BF16),
        ],
        in_specs=[hbm] * 6,
        out_specs=[hbm] * 6,
        scratch_shapes=[
            pltpu.VMEM((PAIR, WIDE), BF16),
            pltpu.VMEM((PAIR, WIDE), BF16),
            pltpu.VMEM((PAIR, D), BF16),
            pltpu.VMEM((PAIR, D), BF16),
            pltpu.VMEM((8, 1, BLK), jnp.int32),
            pltpu.VMEM((COLS, D), BF16),
            pltpu.VMEM((COLS, D), BF16),
            pltpu.VMEM((COLS // 2, D), BF16),
            pltpu.VMEM((COLS // 2, D), BF16),
            pltpu.VMEM((4 * PAIR, 2 * D), BF16),
            pltpu.VMEM((BLK, 2 * D), BF16),
            pltpu.VMEM((2, 4 * PAIR, BLK), F32),
            pltpu.VMEM((4, 8, PAIR, PAIR), F32),
            pltpu.VMEM((4, 8, PAIR, PAIR), F32),
            pltpu.VMEM((4, 8, 8, PAIR), F32),
            pltpu.VMEM((4, 8, 8, PAIR), F32),
            pltpu.VMEM((4, 8, 8, PAIR), F32),
            pltpu.VMEM((4, 8, 8, PAIR), F32),
            pltpu.VMEM((8, 8, PAIR), F32),
            pltpu.VMEM((PAIR, COLS), BF16),
            pltpu.VMEM((4 * PAIR, COLS), BF16),
            pltpu.VMEM((D, 4 * PAIR), BF16),
            pltpu.VMEM((2, 2, BLK, 2 * D), F32),
            pltpu.VMEM((3, 2, BLK, 2 * D), BF16),
            pltpu.VMEM((2, 2, BLK, 2 * D), BF16),
            pltpu.VMEM((BLK, 2 * D), F32),
            pltpu.VMEM((BLK, 2 * D), F32),
            pltpu.VMEM((2, BLK, WIDE), BF16),
            pltpu.SMEM((2 * count,), jnp.int32),
            pltpu.VMEM((PIECE, 2 * D), BF16),
            pltpu.SemaphoreType.DMA((6,)),
            pltpu.SemaphoreType.DMA((3, 2, PIECES)),
            pltpu.SemaphoreType.DMA((3, 2, PIECES)),
            pltpu.SemaphoreType.DMA((5,)),
            pltpu.SemaphoreType.DMA((5,)),
            pltpu.SemaphoreType.DMA((3, 2, PIECES)),
            pltpu.SemaphoreType.DMA((3, 2, PIECES)),
            pltpu.SemaphoreType.DMA((2,)),
        ],
        compiler_params=pltpu.CompilerParams(
            collective_id=0, has_side_effects=True, vmem_limit_bytes=60 * 1024 * 1024
        ),
        name="attention_backward",
    )(block_order, docs, queries, key_states, value_states, grad_output)
    return pl.pallas_call(
        functools.partial(last_kernel, count, inner),
        out_shape=[
            jax.ShapeDtypeStruct((PAIR, WIDE), BF16),
            jax.ShapeDtypeStruct((PAIR, D), BF16),
            jax.ShapeDtypeStruct((PAIR, D), BF16),
        ],
        in_specs=[hbm] * 7,
        out_specs=[hbm] * 3,
        scratch_shapes=[
            pltpu.VMEM((2, BLK, WIDE), BF16),
            pltpu.VMEM((2, BLK, 2 * D), F32),
            pltpu.VMEM((2, BLK, 2 * D), BF16),
            pltpu.VMEM((2, BLK, D), BF16),
            pltpu.VMEM((2, BLK, D), BF16),
            pltpu.SMEM((2 * count,), jnp.int32),
            pltpu.SemaphoreType.DMA((7,)),
            pltpu.SemaphoreType.DMA((6,)),
        ],
        name="stored_order",
    )(block_order, *mid)


def solution(mesh):
    rows = P(("outer", "inner"), None)
    return jax.shard_map(
        on_device,
        mesh=mesh,
        in_specs=(rows, rows, rows, rows, P(), P()),
        out_specs=(rows, rows, rows),
        check_vma=False,
    )
```
